32 devices in a mesh: seq: 8 (over y, x, core), tp: 4 (over z).
Axes of the slice: x: 2, y: 2, z: 4, core: 2. Of those that a mesh axis runs over, the one named last changes fastest.
Arguments:
- head_inputs: bfloat16 [8192, 6144], P('seq', 'tp'), may hold values from -2 to 2
- write_keys: bfloat16 [8192, 128], P(('seq', 'tp')), may hold values from -1.796875 to 1.796875
- read_queries: bfloat16 [8192, 128], P(('seq', 'tp')), may hold values from -1.796875 to 1.796875
- log_decay: float32 [96, 8192], P('tp', 'seq'), may hold values from -0.7 to 0
- skip_gain: float32 [96], P('tp'), may hold values from 0.5 to 1.5
- out_grad: bfloat16 [8192, 6144], P('seq', 'tp'), may hold values from -2 to 2
Outputs:
- mixed_out: bfloat16 [8192, 6144], P('seq', 'tp')
- input_grad: bfloat16 [8192, 6144], P('seq', 'tp')
- write_grad: bfloat16 [8192, 128], P(('seq', 'tp'))
- read_grad: bfloat16 [8192, 128], P(('seq', 'tp'))
The draws below stay inside these ranges and needn't reach their ends.
All inputs are finite; a program needn't handle non-finite values.
Results may differ from the reference program's by a relative error of at most 0.015.
Values may be sent and summed in bfloat16 or wider, within the bound.
A program may use at most 128 MiB of HBM per device.

```python
import math
import jax
import jax.numpy as jnp
from jax import lax

HEADS = 96
HEADDIM = 64
STATE = 128
TOK_DEV = 1024
BLK = 512
TOKENS = 8192


def head_rates(key):
    base = jax.random.fold_in(key, 11)
    pick_key, fast_key, slow_key = jax.random.split(base, 3)
    fast_share = 0.5
    slow_low = 0.6 / TOKENS
    slow_high = 6.0 / TOKENS
    chosen = jax.random.uniform(pick_key, (HEADS,)) < fast_share
    fast = jnp.exp(jax.random.uniform(fast_key, (HEADS,), minval=math.log(0.5 / TOK_DEV), maxval=math.log(3.0 / TOK_DEV)))
    slow = jnp.exp(jax.random.uniform(slow_key, (HEADS,), minval=math.log(slow_low), maxval=math.log(slow_high)))
    return jnp.where(chosen, fast, slow)


def scaled_field(key, salt):
    rates = head_rates(key)
    column_scale = jnp.repeat(jnp.sqrt(2.0 * jnp.minimum(rates, 0.05)), HEADDIM)
    local = jax.random.fold_in(key, salt)
    value_key = jax.random.fold_in(local, 0)
    values = jnp.clip(jax.random.normal(value_key, (TOKENS, HEADS * HEADDIM)), -6.0, 6.0)
    return (values * column_scale[None, :]).astype(jnp.bfloat16)


def draw_head_inputs(key, part):
    return scaled_field(key, 31)


def draw_out_grad(key, part):
    return scaled_field(key, 47)


def draw_log_decay(key, part):
    rates = head_rates(key)
    local = jax.random.fold_in(key, 23)
    jitter_key, device_key, spot_key, drop_key = jax.random.split(local, 4)
    jitter = jax.random.uniform(jitter_key, (HEADS, TOKENS), minval=0.5, maxval=1.5)
    spans = TOKENS // TOK_DEV
    device_factor = jnp.exp(jax.random.uniform(device_key, (HEADS, spans), minval=math.log(0.5), maxval=math.log(2.0)))
    device_factor = jnp.repeat(device_factor, TOK_DEV, axis=1)
    token_rates = rates[:, None] * jitter * device_factor
    spots = jax.random.randint(spot_key, (2,), 0, TOKENS)
    struck = jnp.any(jnp.arange(TOKENS)[None, :] == spots[:, None], axis=0)
    drops = jax.random.uniform(drop_key, (HEADS, 1), minval=0.22, maxval=0.69)
    return jnp.where(struck[None, :], -drops, -token_rates).astype(jnp.float32)


def level_of(stream_key, shape, cuts, least, top_value):
    def one(position, parts):
        steps = jax.random.uniform(jax.random.fold_in(jax.random.fold_in(stream_key, 6), position), (parts,), jnp.float32, least / len(cuts), top_value / len(cuts))
        return jnp.repeat(jnp.exp(steps), shape[position] // parts).reshape((-1,) + (1,) * (len(shape) - position - 1))

    factor_of = one(*cuts[0])
    for cut in cuts[1:]:
        factor_of = factor_of * one(*cut)
    return factor_of


def scatter_about(key, dims, scale, reach, shards=(), kind=jnp.bfloat16):
    loudness = level_of(key, dims, shards, -0.22, 0.18) if shards else 1.0
    values = jax.random.normal(key, dims, jnp.float32) * scale * loudness
    return jnp.minimum(jnp.maximum(values, -reach), reach).astype(kind)


def setup_inputs(seed: int = 0) -> dict:
    key_of = jax.random.split(jax.random.key(seed), 7)
    head_inputs = draw_head_inputs(jax.random.fold_in(key_of[6], 71), 0)
    write_keys = scatter_about(key_of[1], (TOKENS, STATE), 0.3, 1.796875, ((0, 32),))
    read_queries = scatter_about(key_of[2], (TOKENS, STATE), 0.3, 1.796875, ((0, 32),))
    log_decay = draw_log_decay(jax.random.fold_in(key_of[6], 71), 0)
    skip_gain = jnp.clip(0.5 + 1.0 * jax.random.uniform(key_of[4], (HEADS,), jnp.float32) ** level_of(key_of[4], (HEADS,), ((0, 4),), -0.2, 0.2), 0.5, 1.5)
    out_grad = draw_out_grad(jax.random.fold_in(key_of[6], 71), 0)
    return {"head_inputs": head_inputs, "write_keys": write_keys, "read_queries": read_queries, "log_decay": log_decay, "skip_gain": skip_gain, "out_grad": out_grad}


def repeat_heads(values):
    return jnp.repeat(values, HEADDIM, axis=-1)


def block_pieces(running_b, input_b, grad_b, key_b, query_b):
    order = jnp.arange(BLK)
    lower = order[:, None] >= order[None, :]
    gram = jnp.dot(query_b, key_b.T, preferred_element_type=jnp.float32)
    spread = running_b[:, :, None] - running_b[:, None, :]
    decay = jnp.exp(jnp.where(lower[None], spread, -jnp.inf))
    weights = (decay * gram[None]).astype(jnp.bfloat16)
    to_end = repeat_heads(jnp.exp(running_b[:, -1:] - running_b).T)
    from_start = repeat_heads(jnp.exp(running_b).T)
    scaled_in = (input_b.astype(jnp.float32) * to_end).astype(jnp.bfloat16)
    scaled_grad = (grad_b.astype(jnp.float32) * from_start).astype(jnp.bfloat16)
    input_heads = input_b.reshape(BLK, HEADS, HEADDIM).astype(jnp.float32)
    grad_heads = grad_b.reshape(BLK, HEADS, HEADDIM).astype(jnp.float32)
    pairs = jnp.einsum("thp,shp->hts", grad_heads, input_heads)
    mixer = jnp.sum(decay * pairs, axis=0)
    return weights, mixer, to_end, from_start, scaled_in, scaled_grad, input_heads, grad_heads


def reference(head_inputs, write_keys, read_queries, log_decay, skip_gain, out_grad):
    width = HEADS * HEADDIM
    blocks = TOKENS // BLK
    input_blocks = head_inputs.reshape(blocks, BLK, width)
    grad_blocks = out_grad.reshape(blocks, BLK, width)
    key_blocks = write_keys.reshape(blocks, BLK, STATE)
    query_blocks = read_queries.reshape(blocks, BLK, STATE)
    running = jnp.cumsum(log_decay.reshape(HEADS, blocks, BLK), axis=2).transpose(1, 0, 2)
    skip_cols = repeat_heads(skip_gain)

    def forward_step(state, pack):
        running_b, input_b, grad_b, key_b, query_b = pack
        weights, mixer, to_end, from_start, scaled_in, scaled_grad, input_heads, grad_heads = block_pieces(running_b, input_b, grad_b, key_b, query_b)
        state_low = state.astype(jnp.bfloat16)
        inner = jnp.einsum("hts,shp->thp", weights.astype(jnp.float32), input_heads).reshape(BLK, width)
        carried = jnp.dot(query_b, state_low, preferred_element_type=jnp.float32) * from_start
        mixed = (inner + carried + skip_cols[None, :] * input_b.astype(jnp.float32)).astype(jnp.bfloat16)
        query_grad = jnp.dot(mixer, key_b.astype(jnp.float32), precision=lax.Precision.HIGHEST)
        query_grad = query_grad + jnp.dot(scaled_grad, state_low.T, preferred_element_type=jnp.float32)
        summary = jnp.dot(key_b.T, scaled_in, preferred_element_type=jnp.float32)
        new_state = jnp.exp(repeat_heads(running_b[:, -1]))[None, :] * state + summary
        return new_state, (mixed, query_grad.astype(jnp.bfloat16))

    def backward_step(cot, pack):
        running_b, input_b, grad_b, key_b, query_b = pack
        weights, mixer, to_end, from_start, scaled_in, scaled_grad, input_heads, grad_heads = block_pieces(running_b, input_b, grad_b, key_b, query_b)
        cot_low = cot.astype(jnp.bfloat16)
        inner = jnp.einsum("hts,thp->shp", weights.astype(jnp.float32), grad_heads).reshape(BLK, width)
        carried = jnp.dot(key_b, cot_low, preferred_element_type=jnp.float32) * to_end
        in_grad = (inner + carried + skip_cols[None, :] * grad_b.astype(jnp.float32)).astype(jnp.bfloat16)
        key_grad = jnp.dot(mixer.T, query_b.astype(jnp.float32), precision=lax.Precision.HIGHEST)
        key_grad = key_grad + jnp.dot(scaled_in, cot_low.T, preferred_element_type=jnp.float32)
        summary = jnp.dot(query_b.T, scaled_grad, preferred_element_type=jnp.float32)
        new_cot = jnp.exp(repeat_heads(running_b[:, -1]))[None, :] * cot + summary
        return new_cot, (in_grad, key_grad.astype(jnp.bfloat16))

    packs = (running, input_blocks, grad_blocks, key_blocks, query_blocks)
    empty = jnp.zeros((STATE, width), jnp.float32)
    unused_state, forward_outs = lax.scan(forward_step, empty, packs)
    unused_cot, backward_outs = lax.scan(backward_step, empty, packs, reverse=True)
    mixed_out = forward_outs[0].reshape(TOKENS, width)
    read_grad = forward_outs[1].reshape(TOKENS, STATE)
    input_grad = backward_outs[0].reshape(TOKENS, width)
    write_grad = backward_outs[1].reshape(TOKENS, STATE)
    return (mixed_out, input_grad, write_grad, read_grad)
```

```python
import functools
import jax
import jax.numpy as jnp
import numpy as np
from jax import lax
from jax.experimental import pallas as pl
from jax.experimental.pallas import tpu as pltpu
from jax.sharding import PartitionSpec as P

HEADDIM = 64
CHUNK = 128
HALF = CHUNK // 2
PIECES = 4
MESH = pl.DeviceIdType.MESH
F32 = jnp.float32
BF16 = jnp.bfloat16
LIMIT = 56 * 1024 * 1024
NT = (((1,), (1,)), ((), ()))
TN = (((0,), (0,)), ((), ()))


def exact_nt(a, b):
    return lax.dot_general(a, b, NT, precision=lax.Precision.HIGHEST, preferred_element_type=F32)


def widen(values, spread, heads):
    high = values.astype(BF16)
    low = (values - high.astype(F32)).astype(BF16)
    lane = lax.broadcasted_iota(jnp.int32, values.shape, 1)
    both = jnp.where(lane < heads, high.astype(F32), low.astype(F32)).astype(BF16)
    return jnp.dot(both, spread, preferred_element_type=F32)


def about_middle():
    row = lax.broadcasted_iota(jnp.int32, (CHUNK + 8, CHUNK), 0)
    col = lax.broadcasted_iota(jnp.int32, (CHUNK + 8, CHUNK), 1)
    first = jnp.where(col < HALF, 1.0, 0.0)
    inner = jnp.where(col <= row, 1.0, 0.0) - first
    tail = jnp.where(row == CHUNK, first, jnp.where(row == CHUNK + 1, 1.0 - first, 0.0))
    return jnp.where(row < CHUNK, inner, tail)


def gather_kernel(
    nseq, ntp, heads,
    x_ref, g_ref, k_ref, q_ref, ld_ref, e_ref,
    xs_ref, gs_ref, kout_ref, qout_ref, sin_ref, cin_ref,
    kbuf, qbuf, tsum, csum, factors, srecv, crecv, ssend, csend,
    ag_send, ag_recv, st_send, st_recv, ct_send, ct_recv,
):
    seq, tp = lax.axis_index("seq"), lax.axis_index("tp")
    rows = k_ref.shape[0]
    chunks = x_ref.shape[0] // CHUNK
    per = rows // CHUNK
    right, left = lax.rem(seq + 1, nseq), lax.rem(seq + nseq - 1, nseq)

    barrier = pltpu.get_barrier_semaphore()
    for k in range(1, ntp):
        pl.semaphore_signal(
            barrier, inc=1, device_id={"tp": lax.rem(tp + k, ntp)}, device_id_type=MESH
        )
    for other in (left, right):
        pl.semaphore_signal(barrier, inc=1, device_id={"seq": other}, device_id_type=MESH)
    pl.semaphore_wait(barrier, ntp - 1 + 2)

    def ag_copy(which, k, place):
        src, dst = ((k_ref, kbuf), (q_ref, qbuf))[which]
        return pltpu.make_async_remote_copy(
            src_ref=src,
            dst_ref=dst.at[pl.ds(pl.multiple_of(place * rows, rows), rows)],
            send_sem=ag_send.at[which, k],
            recv_sem=ag_recv.at[which, k],
            device_id={"tp": lax.rem(tp + k, ntp)},
            device_id_type=MESH,
        )

    for k in range(ntp - 1, 0, -1):
        for which in range(2):
            ag_copy(which, k, tp).start()

    own = pl.ds(pl.multiple_of(tp * rows, rows), rows)
    kbuf[own, :] = k_ref[...]
    qbuf[own, :] = q_ref[...]

    spread = e_ref[...]
    tokens = x_ref.shape[0]
    row = lax.broadcasted_iota(jnp.int32, (chunks, tokens), 0)
    col = lax.broadcasted_iota(jnp.int32, (chunks, tokens), 1)
    before = jnp.where(col < row * CHUNK + HALF, 1.0, 0.0)
    logs = ld_ref[...]
    sums = jnp.concatenate(
        [
            exact_nt(1.0 - before, logs),
            exact_nt(before, logs),
            exact_nt(jnp.ones((chunks, tokens), F32), logs),
        ],
        axis=0,
    )
    factors[...] = widen(jnp.exp(sums), spread, heads)

    def scale(c, carry):
        at = pl.ds(pl.multiple_of(c * CHUNK, CHUNK), CHUNK)
        d = exact_nt(about_middle()[:CHUNK], ld_ref[:, at])
        a = widen(jnp.exp(-d), spread, heads)
        xs_ref[at, :] = (x_ref[at, :].astype(F32) * a).astype(BF16)
        b = widen(jnp.exp(d), spread, heads)
        gs_ref[at, :] = (g_ref[at, :].astype(F32) * b).astype(BF16)
        return carry

    lax.fori_loop(0, chunks, scale, 0)

    tsum[...] = jnp.zeros_like(tsum)
    csum[...] = jnp.zeros_like(csum)

    def add_chunk(c):
        at = pl.ds(pl.multiple_of(c * CHUNK, CHUNK), CHUNK)
        up = lax.dot_general(kbuf[at, :], xs_ref[at, :], TN, preferred_element_type=F32)
        tsum[...] += factors[pl.ds(c, 1), :] * up
        down = lax.dot_general(qbuf[at, :], gs_ref[at, :], TN, preferred_element_type=F32)
        csum[...] += factors[pl.ds(chunks + c, 1), :] * down

    for k in range(ntp):
        place = lax.rem(tp - k + ntp, ntp)
        if k > 0:
            for which in range(2):
                ag_copy(which, k, place).wait_recv()

        def one(j, carry, place=place):
            add_chunk(place * per + j)
            return carry

        lax.fori_loop(0, per, one, 0)

    whole = factors[2 * chunks : 2 * chunks + 1, :]
    step = tsum.shape[0] // PIECES

    def chain(own_sum, got, out, send, recv, first, last, nxt):
        @pl.when(seq == first)
        def _():
            got[...] = jnp.zeros_like(got)

        def piece(p, carry):
            at = pl.ds(pl.multiple_of(p * step, step), step)
            copy = pltpu.make_async_remote_copy(
                src_ref=out.at[at],
                dst_ref=got.at[at],
                send_sem=send.at[p],
                recv_sem=recv.at[p],
                device_id={"seq": nxt},
                device_id_type=MESH,
            )

            @pl.when(seq != first)
            def _():
                copy.wait_recv()

            @pl.when(seq != last)
            def _():
                out[at, :] = (whole * got[at, :].astype(F32) + own_sum[at, :]).astype(BF16)
                copy.start()

            return carry

        lax.fori_loop(0, PIECES, piece, 0)

    def states():
        chain(tsum, srecv, ssend, st_send, st_recv, 0, nseq - 1, right)

    def cotangents():
        chain(csum, crecv, csend, ct_send, ct_recv, nseq - 1, 0, left)

    early = 2 * seq < nseq

    @pl.when(early)
    def _():
        states()
        cotangents()

    @pl.when(jnp.logical_not(early))
    def _():
        cotangents()
        states()

    kout_ref[...] = kbuf[...]
    qout_ref[...] = qbuf[...]
    sin_ref[...] = srecv[...]
    cin_ref[...] = crecv[...]

    def drain(out, got, send, recv, nxt, last):
        @pl.when(seq != last)
        def _():
            for p in range(PIECES):
                at = pl.ds(p * step, step)
                pltpu.make_async_remote_copy(
                    src_ref=out.at[at], dst_ref=got.at[at], send_sem=send.at[p], recv_sem=recv.at[p],
                    device_id={"seq": nxt}, device_id_type=MESH,
                ).wait_send()

    drain(ssend, srecv, st_send, st_recv, right, nseq - 1)
    drain(csend, crecv, ct_send, ct_recv, left, 0)
    for k in range(1, ntp):
        for which in range(2):
            ag_copy(which, k, tp).wait_send()


def main_kernel(
    heads,
    xf, gf, kf, qf, xb, gb, kb, qb, ld_ref, e_ref, skip_ref, s_in, c_in,
    mixed_ref, grad_ref, read_ref, write_ref,
    state, cot, fstack, bstack,
):
    i = pl.program_id(0)
    n = pl.num_programs(0)
    j = n - 1 - i

    @pl.when(i == 0)
    def _():
        state[...] = s_in[...].astype(F32)
        cot[...] = c_in[...].astype(F32)

    spread = e_ref[...]
    middle = about_middle()
    skip = widen(jnp.broadcast_to(skip_ref[...], (8, skip_ref.shape[1])), spread, heads)[0:1, :]
    row = lax.broadcasted_iota(jnp.int32, (CHUNK, CHUNK), 0)
    col = lax.broadcasted_iota(jnp.int32, (CHUNK, CHUNK), 1)
    lower, upper = row >= col, row <= col

    def one(c, flip, left, keys, x, g, stack, carry):
        at = pl.ds(pl.multiple_of(c * CHUNK, CHUNK), CHUNK)
        d = exact_nt(middle, ld_ref[:, at])
        srow = lax.broadcasted_iota(jnp.int32, d.shape, 0)
        if flip:
            d = jnp.where(srow < CHUNK, -d, d)
        factor = widen(jnp.exp(d), spread, heads)
        outer = factor[:CHUNK]
        first, second = factor[CHUNK : CHUNK + 1], factor[CHUNK + 1 : CHUNK + 2]
        if flip:
            first, second = second, first
        mask = upper if flip else lower
        gram = lax.dot_general(left, keys, NT, preferred_element_type=F32)
        gram = jnp.where(mask, gram, 0.0).astype(BF16)
        low = first * carry[...]
        stack[0:CHUNK, :] = x
        stack[CHUNK:, :] = low.astype(BF16)
        total = jnp.dot(
            jnp.concatenate([gram, left], axis=1), stack[...], preferred_element_type=F32
        )
        out = (outer * (total + skip * x.astype(F32))).astype(BF16)
        both = lax.dot_general(g, stack[...], NT, preferred_element_type=F32)
        mixer = jnp.where(mask, both[:, :CHUNK], 0.0).astype(BF16)
        small = jnp.dot(mixer, keys, preferred_element_type=F32) + both[:, CHUNK:]
        carry[...] = second * (low + lax.dot_general(keys, x, TN, preferred_element_type=F32))
        return out, small.astype(BF16)

    mixed_ref[...], read_ref[...] = one(
        i, False, qf[...], kf[...], xf[...], gf[...], fstack, state
    )
    grad_ref[...], write_ref[...] = one(
        j, True, kb[...], qb[...], gb[...], xb[...], bstack, cot
    )


def scatter_kernel(ntp, w_ref, r_ref, wout, rout, got, send, recv):
    tp = lax.axis_index("tp")
    rows = wout.shape[0]
    barrier = pltpu.get_barrier_semaphore()
    for k in range(1, ntp):
        pl.semaphore_signal(
            barrier, inc=1, device_id={"tp": lax.rem(tp + k, ntp)}, device_id_type=MESH
        )
    pl.semaphore_wait(barrier, ntp - 1)

    def copy(which, k):
        src = (w_ref, r_ref)[which]
        peer = lax.rem(tp + k, ntp)
        return pltpu.make_async_remote_copy(
            src_ref=src.at[pl.ds(pl.multiple_of(peer * rows, rows), rows)],
            dst_ref=got.at[which, k - 1],
            send_sem=send.at[which, k],
            recv_sem=recv.at[which, k],
            device_id={"tp": peer},
            device_id_type=MESH,
        )

    for k in range(ntp - 1, 0, -1):
        for which in range(2):
            copy(which, k).start()
    own = pl.ds(pl.multiple_of(tp * rows, rows), rows)
    for which, (src, out) in enumerate(((w_ref, wout), (r_ref, rout))):
        total = src[own, :].astype(F32)
        for k in range(1, ntp):
            copy(which, k).wait_recv()
            total = total + got[which, k - 1].astype(F32)
        out[...] = total.astype(BF16)
    for k in range(1, ntp):
        for which in range(2):
            copy(which, k).wait_send()


def local(nseq, ntp, head_inputs, write_keys, read_queries, log_decay, skip_gain, out_grad):
    tokens, width = head_inputs.shape
    heads = width // HEADDIM
    rows, size = write_keys.shape
    chunks = tokens // CHUNK
    place = np.arange(2 * heads)[:, None] % heads == np.arange(width)[None, :] // HEADDIM
    spread = jnp.asarray(place.astype(np.float32), BF16)
    logs = jnp.concatenate([log_decay, log_decay], axis=0)
    skip = jnp.concatenate([skip_gain, skip_gain])[None, :]
    vmem = pl.BlockSpec(memory_space=pltpu.VMEM)
    dma = pltpu.SemaphoreType.DMA
    big = jax.ShapeDtypeStruct((tokens, width), BF16)
    small = jax.ShapeDtypeStruct((tokens, size), BF16)
    edge = jax.ShapeDtypeStruct((size, width), BF16)
    xs, gs, keys, queries, s_in, c_in = pl.pallas_call(
        functools.partial(gather_kernel, nseq, ntp, heads),
        out_shape=(big, big, small, small, edge, edge),
        in_specs=[vmem] * 6,
        out_specs=[vmem] * 6,
        scratch_shapes=[
            pltpu.VMEM((tokens, size), BF16),
            pltpu.VMEM((tokens, size), BF16),
            pltpu.VMEM((size, width), F32),
            pltpu.VMEM((size, width), F32),
            pltpu.VMEM((3 * chunks, width), F32),
            pltpu.VMEM((size, width), BF16),
            pltpu.VMEM((size, width), BF16),
            pltpu.VMEM((size, width), BF16),
            pltpu.VMEM((size, width), BF16),
            dma((2, ntp)),
            dma((2, ntp)),
            dma((PIECES,)),
            dma((PIECES,)),
            dma((PIECES,)),
            dma((PIECES,)),
        ],
        compiler_params=pltpu.CompilerParams(
            collective_id=0, has_side_effects=True, vmem_limit_bytes=LIMIT
        ),
        name="gather_states",
    )(head_inputs, out_grad, write_keys, read_queries, logs, spread)

    def fwd(block):
        return pl.BlockSpec(block, lambda i: (i, 0))

    def bwd(block):
        return pl.BlockSpec(block, lambda i: (chunks - 1 - i, 0))

    def full(shape):
        return pl.BlockSpec(shape, lambda i: (0, 0))

    wide, thin = (CHUNK, width), (CHUNK, size)
    mixed, grad, read, write = pl.pallas_call(
        functools.partial(main_kernel, heads),
        grid=(chunks,),
        out_shape=(big, big, small, small),
        in_specs=[fwd(wide), fwd(wide), fwd(thin), fwd(thin)]
        + [bwd(wide), bwd(wide), bwd(thin), bwd(thin)]
        + [full(logs.shape), full(spread.shape), full(skip.shape), full((size, width)), full((size, width))],
        out_specs=[fwd(wide), bwd(wide), fwd(thin), bwd(thin)],
        scratch_shapes=[
            pltpu.VMEM((size, width), F32),
            pltpu.VMEM((size, width), F32),
            pltpu.VMEM((CHUNK + size, width), BF16),
            pltpu.VMEM((CHUNK + size, width), BF16),
        ],
        compiler_params=pltpu.CompilerParams(vmem_limit_bytes=LIMIT),
        name="outputs",
    )(xs, gs, keys, queries, xs, gs, keys, queries, logs, spread, skip, s_in, c_in)

    part = jax.ShapeDtypeStruct((rows, size), BF16)
    write_grad, read_grad = pl.pallas_call(
        functools.partial(scatter_kernel, ntp),
        out_shape=(part, part),
        in_specs=[vmem, vmem],
        out_specs=[vmem, vmem],
        scratch_shapes=[
            pltpu.VMEM((2, ntp - 1, rows, size), BF16),
            dma((2, ntp)),
            dma((2, ntp)),
        ],
        compiler_params=pltpu.CompilerParams(collective_id=1, has_side_effects=True),
        name="scatter_grads",
    )(write, read)
    return mixed, grad, write_grad, read_grad


def solution(mesh):
    in_specs = (
        P("seq", "tp"),
        P(("seq", "tp"), None),
        P(("seq", "tp"), None),
        P("tp", "seq"),
        P("tp"),
        P("seq", "tp"),
    )
    out_specs = (P("seq", "tp"), P("seq", "tp"), P(("seq", "tp"), None), P(("seq", "tp"), None))
    body = functools.partial(local, mesh.shape["seq"], mesh.shape["tp"])
    return jax.shard_map(body, mesh=mesh, in_specs=in_specs, out_specs=out_specs, check_vma=False)
```

```python
import functools
import jax
import jax.numpy as jnp
from jax import lax
from jax.experimental import pallas as pl
from jax.experimental.pallas import tpu as pltpu
from jax.sharding import PartitionSpec as P

CHUNK = 128
HALF = CHUNK // 2
LANES = 128
PIECES = 8
MESH = pl.DeviceIdType.MESH
F32 = jnp.float32
BF16 = jnp.bfloat16
LIMIT = 56 * 1024 * 1024
NT = (((1,), (1,)), ((), ()))
TN = (((0,), (0,)), ((), ()))


def exact_nt(a, b):
    return lax.dot_general(a, b, NT, precision=lax.Precision.HIGHEST, preferred_element_type=F32)


def widen(values, width):
    rows, heads = values.shape
    dim = width // heads
    each = LANES // dim
    lane = lax.broadcasted_iota(jnp.int32, (rows, LANES), 1)
    tiles = []
    for p in range(width // LANES):
        tile = jnp.broadcast_to(values[:, p * each : p * each + 1], (rows, LANES))
        for e in range(1, each):
            h = p * each + e
            nxt = jnp.broadcast_to(values[:, h : h + 1], (rows, LANES))
            tile = jnp.where(lane >= e * dim, nxt, tile)
        tiles.append(tile)
    return jnp.concatenate(tiles, axis=1)


def rows_at(c, size):
    return pl.ds(pl.multiple_of(c * size, size), size)


def kernel(
    nseq, ntp,
    x_hbm, g_hbm, k_ref, q_ref, ld_ref, skip_ref,
    mixed_hbm, grad_hbm, wout, rout,
    x_ref, g_ref, xs_ref, gs_ref, xe_ref, ge_ref, kbuf, qbuf, tsum, csum, factors, ea_ref, eb_ref,
    srecv, crecv, ssend, csend, fstack, bstack, wpart, rpart, got,
    load_sem, store_sem, ag_send, ag_recv, st_send, st_recv, ct_send, ct_recv, rs_send, rs_recv,
):
    seq, tp = lax.axis_index("seq"), lax.axis_index("tp")
    rows = k_ref.shape[0]
    tokens, width = x_ref.shape
    chunks = tokens // CHUNK
    per = rows // CHUNK
    right, left = lax.rem(seq + 1, nseq), lax.rem(seq + nseq - 1, nseq)

    def load(which, c):
        src, dst = ((x_hbm, x_ref), (g_hbm, g_ref))[which]
        at = rows_at(c, CHUNK)
        return pltpu.make_async_copy(src.at[at], dst.at[at], load_sem.at[which, c])

    def start_loads(c, carry):
        load(0, c).start()
        load(1, c).start()
        return carry

    lax.fori_loop(0, chunks, start_loads, 0)

    barrier = pltpu.get_barrier_semaphore()
    for k in range(1, ntp):
        pl.semaphore_signal(
            barrier, inc=1, device_id={"tp": lax.rem(tp + k, ntp)}, device_id_type=MESH
        )
    for other in (left, right):
        pl.semaphore_signal(barrier, inc=1, device_id={"seq": other}, device_id_type=MESH)
    pl.semaphore_wait(barrier, ntp - 1 + 2)

    def ag_copy(which, k, place):
        src, dst = ((k_ref, kbuf), (q_ref, qbuf))[which]
        return pltpu.make_async_remote_copy(
            src_ref=src,
            dst_ref=dst.at[rows_at(place, rows)],
            send_sem=ag_send.at[which, k],
            recv_sem=ag_recv.at[which, k],
            device_id={"tp": lax.rem(tp + k, ntp)},
            device_id_type=MESH,
        )

    for k in range(ntp - 1, 0, -1):
        for which in range(2):
            ag_copy(which, k, tp).start()

    own = rows_at(tp, rows)
    kbuf[own, :] = k_ref[...]
    qbuf[own, :] = q_ref[...]

    row = lax.broadcasted_iota(jnp.int32, (chunks, tokens), 0) * CHUNK
    col = lax.broadcasted_iota(jnp.int32, (chunks, tokens), 1)
    before = jnp.where(col < row + HALF, 1.0, 0.0)
    logs = ld_ref[...]
    kinds = (
        1.0 - before,
        before,
        jnp.ones((chunks, tokens), F32),
        jnp.where(col >= row, before, 0.0),
        jnp.where(col < row + CHUNK, 1.0 - before, 0.0),
    )
    for n, kind in enumerate(kinds):
        factors[n * chunks : (n + 1) * chunks, :] = widen(jnp.exp(exact_nt(kind, logs)), width)

    def factor(n, c):
        return factors[pl.ds(n * chunks + c, 1), :]

    trow = lax.broadcasted_iota(jnp.int32, (CHUNK, CHUNK), 0)
    tcol = lax.broadcasted_iota(jnp.int32, (CHUNK, CHUNK), 1)
    lower, upper = trow >= tcol, trow <= tcol
    about_middle = jnp.where(lower, 1.0, 0.0) - jnp.where(tcol < HALF, 1.0, 0.0)

    def scale(c, carry):
        at = rows_at(c, CHUNK)
        d = exact_nt(about_middle, ld_ref[:, at])
        a, b = jnp.exp(-d), jnp.exp(d)
        ea_ref[at, :] = a
        eb_ref[at, :] = b
        load(0, c).wait()
        x = x_ref[at, :].astype(F32) * widen(a, width)
        xs_ref[at, :] = x.astype(BF16)
        xe_ref[at, :] = (x * factor(0, c)).astype(BF16)
        load(1, c).wait()
        g = g_ref[at, :].astype(F32) * widen(b, width)
        gs_ref[at, :] = g.astype(BF16)
        ge_ref[at, :] = (g * factor(1, c)).astype(BF16)
        return carry

    lax.fori_loop(0, chunks, scale, 0)

    for k in range(ntp):
        place = lax.rem(tp - k + ntp, ntp)
        if k > 0:
            for which in range(2):
                ag_copy(which, k, place).wait_recv()
        at = rows_at(place, rows)
        up = lax.dot_general(kbuf[at, :], xe_ref[at, :], TN, preferred_element_type=F32)
        down = lax.dot_general(qbuf[at, :], ge_ref[at, :], TN, preferred_element_type=F32)
        if k == 0:
            tsum[...] = up
            csum[...] = down
        else:
            tsum[...] += up
            csum[...] += down

    whole = factors[2 * chunks : 2 * chunks + 1, :]
    step = tsum.shape[0] // PIECES

    def hop(p, out, got_ref, send, recv, nxt):
        at = rows_at(p, step)
        return at, pltpu.make_async_remote_copy(
            src_ref=out.at[at],
            dst_ref=got_ref.at[at],
            send_sem=send.at[p],
            recv_sem=recv.at[p],
            device_id={"seq": nxt},
            device_id_type=MESH,
        )

    def chain(own_sum, got_ref, out, send, recv, first, last, nxt):
        @pl.when(seq == first)
        def _():
            got_ref[...] = jnp.zeros_like(got_ref)

        def piece(p, carry):
            at, copy = hop(p, out, got_ref, send, recv, nxt)

            @pl.when(seq != first)
            def _():
                copy.wait_recv()

            @pl.when(seq != last)
            def _():
                out[at, :] = (whole * got_ref[at, :].astype(F32) + own_sum[at, :]).astype(BF16)
                copy.start()

            return carry

        lax.fori_loop(0, PIECES, piece, 0)

    def states():
        chain(tsum, srecv, ssend, st_send, st_recv, 0, nseq - 1, right)

    def cotangents():
        chain(csum, crecv, csend, ct_send, ct_recv, nseq - 1, 0, left)

    early = 2 * seq < nseq

    @pl.when(early)
    def _():
        states()
        cotangents()

    @pl.when(jnp.logical_not(early))
    def _():
        cotangents()
        states()

    tsum[...] = srecv[...].astype(F32)
    csum[...] = crecv[...].astype(F32)

    skip = widen(jnp.broadcast_to(skip_ref[...], (8, skip_ref.shape[1])), width)[0:1, :]

    def one(c, flip, left_ref, right_ref, a_ref, b_ref, outer_ref, stack, carry, out, small):
        at = rows_at(c, CHUNK)
        lhs, rhs = left_ref[at, :], right_ref[at, :]
        x = a_ref[at, :]
        first, second = (factor(4, c), factor(3, c)) if flip else (factor(3, c), factor(4, c))
        mask = upper if flip else lower
        gram = lax.dot_general(lhs, rhs, NT, preferred_element_type=F32)
        gram = jnp.where(mask, gram, 0.0).astype(BF16)
        low = first * carry[...]
        stack[0:CHUNK, :] = x
        stack[CHUNK:, :] = low.astype(BF16)
        turned = rhs.astype(F32).T.astype(BF16)
        both = jnp.concatenate(
            [
                jnp.concatenate([gram, lhs], axis=1),
                jnp.concatenate([turned, jnp.zeros((turned.shape[0], lhs.shape[1]), BF16)], axis=1),
            ],
            axis=0,
        )
        result = jnp.dot(both, stack[...], preferred_element_type=F32)
        outer = widen(outer_ref[at, :], width)
        out[at, :] = (outer * (result[:CHUNK] + skip * x.astype(F32))).astype(BF16)
        carry[...] = second * (low + result[CHUNK:])
        pair = lax.dot_general(b_ref[at, :], stack[...], NT, preferred_element_type=F32)
        mixer = jnp.where(mask, pair[:, :CHUNK], 0.0).astype(BF16)
        small[at, :] = (
            jnp.dot(mixer, rhs, preferred_element_type=F32) + pair[:, CHUNK:]
        ).astype(BF16)

    def store(which, c):
        src, dst = ((xe_ref, mixed_hbm), (ge_ref, grad_hbm))[which]
        at = rows_at(c, CHUNK)
        return pltpu.make_async_copy(src.at[at], dst.at[at], store_sem.at[which, c])

    def rs_copy(which, k, j, c, peer):
        src = (rpart, wpart)[which]
        return pltpu.make_async_remote_copy(
            src_ref=src.at[rows_at(c, CHUNK)],
            dst_ref=got.at[which, k - 1, rows_at(j, CHUNK)],
            send_sem=rs_send.at[which, k - 1, j],
            recv_sem=rs_recv.at[which, k - 1, j],
            device_id={"tp": peer},
            device_id_type=MESH,
        )

    def send_part(which, c):
        peer = c // per
        k = lax.rem(peer - tp + ntp, ntp)

        @pl.when(k != 0)
        def _():
            rs_copy(which, k, c - peer * per, c, peer).start()

    def block(i, carry):
        j = chunks - 1 - i
        one(i, False, qbuf, kbuf, xs_ref, gs_ref, eb_ref, fstack, tsum, xe_ref, rpart)
        one(j, True, kbuf, qbuf, gs_ref, xs_ref, ea_ref, bstack, csum, ge_ref, wpart)
        store(0, i).start()
        store(1, j).start()
        send_part(0, i)
        send_part(1, j)
        return carry

    lax.fori_loop(0, chunks, block, 0)

    for which, (src, out) in enumerate(((rpart, rout), (wpart, wout))):
        total = src[own, :].astype(F32)
        for k in range(1, ntp):
            for j in range(per):
                rs_copy(which, k, j, 0, lax.rem(tp + k, ntp)).wait_recv()
            total = total + got[which, k - 1].astype(F32)
        out[...] = total.astype(BF16)

    for k in range(1, ntp):
        for which in range(2):
            ag_copy(which, k, tp).wait_send()
            for j in range(per):
                peer = lax.rem(tp + k, ntp)
                rs_copy(which, k, j, peer * per + j, peer).wait_send()

    def finish(c, carry):
        store(0, c).wait()
        store(1, c).wait()
        return carry

    lax.fori_loop(0, chunks, finish, 0)

    def drain(out, got_ref, send, recv, nxt, last):
        @pl.when(seq != last)
        def _():
            def one_piece(p, carry):
                hop(p, out, got_ref, send, recv, nxt)[1].wait_send()
                return carry

            lax.fori_loop(0, PIECES, one_piece, 0)

    drain(ssend, srecv, st_send, st_recv, right, nseq - 1)
    drain(csend, crecv, ct_send, ct_recv, left, 0)


def local(nseq, ntp, head_inputs, write_keys, read_queries, log_decay, skip_gain, out_grad):
    tokens, width = head_inputs.shape
    rows, size = write_keys.shape
    heads = log_decay.shape[0]
    chunks = tokens // CHUNK
    vmem = pl.BlockSpec(memory_space=pltpu.VMEM)
    hbm = pl.BlockSpec(memory_space=pl.ANY)
    dma = pltpu.SemaphoreType.DMA
    big = jax.ShapeDtypeStruct((tokens, width), BF16)
    part = jax.ShapeDtypeStruct((rows, size), BF16)
    wide, tall = pltpu.VMEM((tokens, width), BF16), pltpu.VMEM((tokens, size), BF16)
    edge, total = pltpu.VMEM((size, width), BF16), pltpu.VMEM((size, width), F32)
    by_head = pltpu.VMEM((tokens, heads), F32)
    stack = pltpu.VMEM((CHUNK + size, width), BF16)
    return pl.pallas_call(
        functools.partial(kernel, nseq, ntp),
        out_shape=(big, big, part, part),
        in_specs=[hbm, hbm, vmem, vmem, vmem, vmem],
        out_specs=[hbm, hbm, vmem, vmem],
        scratch_shapes=[wide] * 6
        + [tall, tall, total, total, pltpu.VMEM((5 * chunks, width), F32), by_head, by_head]
        + [edge] * 4
        + [stack, stack, tall, tall, pltpu.VMEM((2, ntp - 1, rows, size), BF16)]
        + [dma((2, chunks)), dma((2, chunks)), dma((2, ntp)), dma((2, ntp))]
        + [dma((PIECES,))] * 4
        + [dma((2, ntp - 1, rows // CHUNK))] * 2,
        compiler_params=pltpu.CompilerParams(
            collective_id=0, has_side_effects=True, vmem_limit_bytes=LIMIT
        ),
        name="ssd_layer",
    )(head_inputs, out_grad, write_keys, read_queries, log_decay, skip_gain[None, :])


def solution(mesh):
    in_specs = (
        P("seq", "tp"),
        P(("seq", "tp"), None),
        P(("seq", "tp"), None),
        P("tp", "seq"),
        P("tp"),
        P("seq", "tp"),
    )
    out_specs = (P("seq", "tp"), P("seq", "tp"), P(("seq", "tp"), None), P(("seq", "tp"), None))
    body = functools.partial(local, mesh.shape["seq"], mesh.shape["tp"])
    return jax.shard_map(body, mesh=mesh, in_specs=in_specs, out_specs=out_specs, check_vma=False)
```

```python
import functools
import jax
import jax.numpy as jnp
from jax import lax
from jax.experimental import pallas as pl
from jax.experimental.pallas import tpu as pltpu
from jax.sharding import PartitionSpec as P

CHUNK = 128
HALF = CHUNK // 2
LANES = 128
MESH = pl.DeviceIdType.MESH
F32 = jnp.float32
BF16 = jnp.bfloat16
LIMIT = 56 * 1024 * 1024
NT = (((1,), (1,)), ((), ()))
TN = (((0,), (0,)), ((), ()))


def exact_nt(a, b):
    return lax.dot_general(a, b, NT, precision=lax.Precision.HIGHEST, preferred_element_type=F32)


def widen(values, width):
    rows, heads = values.shape
    dim = width // heads
    each = LANES // dim
    lane = lax.broadcasted_iota(jnp.int32, (rows, LANES), 1)
    tiles = []
    for p in range(width // LANES):
        tile = jnp.broadcast_to(values[:, p * each : p * each + 1], (rows, LANES))
        for e in range(1, each):
            h = p * each + e
            nxt = jnp.broadcast_to(values[:, h : h + 1], (rows, LANES))
            tile = jnp.where(lane >= e * dim, nxt, tile)
        tiles.append(tile)
    return jnp.concatenate(tiles, axis=1)


def rows_at(c, size):
    return pl.ds(pl.multiple_of(c * size, size), size)


def kernel(
    nseq, ntp,
    x_hbm, g_hbm, k_ref, q_ref, ld_ref, skip_ref,
    mixed_ref, grad_ref, wout, rout,
    x_ref, g_ref, xs_ref, gs_ref, xe_ref, ge_ref, kbuf, qbuf, tsum, csum, factors, ea_ref, eb_ref,
    logsum, pairfac, corefac, pair_out, pair_in, sums_out, sums_in, half_out, half_in,
    fstack, bstack, wpart, rpart, wlocal, rlocal, got,
    load_sem, ag_send, ag_recv, log_send, log_recv, pair_send, pair_recv, sum_send, sum_recv,
    half_send, half_recv, rs_send, rs_recv,
):
    seq, tp = lax.axis_index("seq"), lax.axis_index("tp")
    rows = k_ref.shape[0]
    tokens, width = x_ref.shape
    chunks = tokens // CHUNK
    per = rows // CHUNK
    groups = nseq // 2
    group = seq // 2
    core = seq - 2 * group
    sibling = 2 * group + 1 - core
    heads = ld_ref.shape[0]

    def load(which, c):
        src, dst = ((x_hbm, x_ref), (g_hbm, g_ref))[which]
        at = rows_at(c, CHUNK)
        return pltpu.make_async_copy(src.at[at], dst.at[at], load_sem.at[which, c])

    def start_loads(c, carry):
        load(0, c).start()
        load(1, c).start()
        return carry

    lax.fori_loop(0, chunks, start_loads, 0)

    barrier = pltpu.get_barrier_semaphore()
    for k in range(1, ntp):
        pl.semaphore_signal(
            barrier, inc=1, device_id={"tp": lax.rem(tp + k, ntp)}, device_id_type=MESH
        )
    for k in range(1, nseq):
        pl.semaphore_signal(
            barrier, inc=1, device_id={"seq": lax.rem(seq + k, nseq)}, device_id_type=MESH
        )
    pl.semaphore_wait(barrier, ntp - 1 + nseq - 1)

    def ag_copy(which, k, place):
        src, dst = ((k_ref, kbuf), (q_ref, qbuf))[which]
        return pltpu.make_async_remote_copy(
            src_ref=src,
            dst_ref=dst.at[rows_at(place, rows)],
            send_sem=ag_send.at[which, k],
            recv_sem=ag_recv.at[which, k],
            device_id={"tp": lax.rem(tp + k, ntp)},
            device_id_type=MESH,
        )

    for k in range(ntp - 1, 0, -1):
        for which in range(2):
            ag_copy(which, k, tp).start()

    own = rows_at(tp, rows)
    kbuf[own, :] = k_ref[...]
    qbuf[own, :] = q_ref[...]

    row = lax.broadcasted_iota(jnp.int32, (chunks, tokens), 0) * CHUNK
    col = lax.broadcasted_iota(jnp.int32, (chunks, tokens), 1)
    before = jnp.where(col < row + HALF, 1.0, 0.0)
    logs = ld_ref[...]
    kinds = (
        1.0 - before,
        before,
        jnp.where(col >= row, before, 0.0),
        jnp.where(col < row + CHUNK, 1.0 - before, 0.0),
    )
    whole_log = exact_nt(jnp.ones((8, tokens), F32), logs)
    logsum[seq] = jnp.zeros((8, logsum.shape[2]), F32)
    logsum[seq, :, 0:heads] = whole_log

    def log_copy(k, place):
        return pltpu.make_async_remote_copy(
            src_ref=logsum.at[place],
            dst_ref=logsum.at[place],
            send_sem=log_send.at[k],
            recv_sem=log_recv.at[k],
            device_id={"seq": lax.rem(seq + k, nseq)},
            device_id_type=MESH,
        )

    for k in range(1, nseq):
        log_copy(k, seq).start()
    for n, kind in enumerate(kinds):
        factors[n * chunks : (n + 1) * chunks, :] = widen(jnp.exp(exact_nt(kind, logs)), width)

    def factor(n, c):
        return factors[pl.ds(n * chunks + c, 1), :]

    trow = lax.broadcasted_iota(jnp.int32, (CHUNK, CHUNK), 0)
    tcol = lax.broadcasted_iota(jnp.int32, (CHUNK, CHUNK), 1)
    lower, upper = trow >= tcol, trow <= tcol
    about_middle = jnp.where(lower, 1.0, 0.0) - jnp.where(tcol < HALF, 1.0, 0.0)

    def scale(c, carry):
        at = rows_at(c, CHUNK)
        d = exact_nt(about_middle, ld_ref[:, at])
        a, b = jnp.exp(-d), jnp.exp(d)
        ea_ref[at, :] = a
        eb_ref[at, :] = b
        load(0, c).wait()
        x = x_ref[at, :].astype(F32) * widen(a, width)
        xs_ref[at, :] = x.astype(BF16)
        xe_ref[at, :] = (x * factor(0, c)).astype(BF16)
        load(1, c).wait()
        g = g_ref[at, :].astype(F32) * widen(b, width)
        gs_ref[at, :] = g.astype(BF16)
        ge_ref[at, :] = (g * factor(1, c)).astype(BF16)
        return carry

    lax.fori_loop(0, chunks, scale, 0)

    for k in range(1, nseq):
        log_copy(k, lax.rem(seq - k + nseq, nseq)).wait_recv()
    for n in range(groups):
        both_logs = logsum[2 * n, :, 0:heads] + logsum[2 * n + 1, :, 0:heads]
        pairfac[8 * n : 8 * n + 8, :] = widen(jnp.exp(both_logs), width)
    for n in range(2):
        corefac[8 * n : 8 * n + 8, :] = widen(jnp.exp(logsum[2 * group + n, :, 0:heads]), width)

    for k in range(ntp):
        place = lax.rem(tp - k + ntp, ntp)
        if k > 0:
            for which in range(2):
                ag_copy(which, k, place).wait_recv()
        at = rows_at(place, rows)
        up = lax.dot_general(kbuf[at, :], xe_ref[at, :], TN, preferred_element_type=F32)
        down = lax.dot_general(qbuf[at, :], ge_ref[at, :], TN, preferred_element_type=F32)
        if k == 0:
            tsum[...] = up
            csum[...] = down
        else:
            tsum[...] += up
            csum[...] += down

    half = tsum.shape[0] // 2
    mine, others = rows_at(core, half), rows_at(1 - core, half)

    def to_sibling(n, src, dst, send, recv):
        return pltpu.make_async_remote_copy(
            src_ref=src.at[n],
            dst_ref=dst.at[n],
            send_sem=send.at[n],
            recv_sem=recv.at[n],
            device_id={"seq": sibling},
            device_id_type=MESH,
        )

    for n, total in enumerate((tsum, csum)):
        pair_out[n] = total[others, :].astype(BF16)
        to_sibling(n, pair_out, pair_in, pair_send, pair_recv).start()
    for n in range(2):
        to_sibling(n, pair_out, pair_in, pair_send, pair_recv).wait_recv()

    fac0, fac1 = corefac[0:1, :], corefac[8:9, :]
    is_first = core == 0

    def ordered(n, total):
        ours, theirs = total[mine, :], pair_in[n].astype(F32)
        return jnp.where(is_first, ours, theirs), jnp.where(is_first, theirs, ours)

    s0, s1 = ordered(0, tsum)
    sums_out[0] = (fac1 * s0 + s1).astype(BF16)
    c0, c1 = ordered(1, csum)
    sums_out[1] = (fac0 * c1 + c0).astype(BF16)

    def sum_copy(n, k, place):
        peer = lax.rem(group + k, groups)
        return pltpu.make_async_remote_copy(
            src_ref=sums_out.at[n],
            dst_ref=sums_in.at[place],
            send_sem=sum_send.at[k],
            recv_sem=sum_recv.at[place],
            device_id={"seq": 2 * peer + core},
            device_id_type=MESH,
        )

    for k in range(1, groups):
        later = group + k < groups

        @pl.when(later)
        def _(k=k):
            sum_copy(0, k, group).start()

        @pl.when(jnp.logical_not(later))
        def _(k=k):
            sum_copy(1, k, group).start()

    def local_grads(c, carry):
        at = rows_at(c, CHUNK)
        mixer = lax.dot_general(gs_ref[at, :], xs_ref[at, :], NT, preferred_element_type=F32)
        mixer = jnp.where(lower, mixer, 0.0).astype(BF16)
        rlocal[at, :] = jnp.dot(mixer, kbuf[at, :], preferred_element_type=F32)
        wlocal[at, :] = lax.dot_general(mixer, qbuf[at, :], TN, preferred_element_type=F32)
        return carry

    lax.fori_loop(0, chunks, local_grads, 0)

    c1_half = jnp.where(is_first, pair_in[1].astype(F32), csum[mine, :])
    s0_half = jnp.where(is_first, tsum[mine, :], pair_in[0].astype(F32))
    csum[mine, :] = jnp.zeros((half, width), F32)
    tsum[mine, :] = jnp.zeros((half, width), F32)
    for order, total, test in (
        (range(groups), tsum, lambda n: n < group),
        (range(groups - 1, -1, -1), csum, lambda n: n > group),
    ):
        for n in order:

            @pl.when(test(n))
            def _(n=n, total=total):
                sum_copy(0, 1, n).wait_recv()
                total[mine, :] = (
                    pairfac[8 * n : 8 * n + 1, :] * total[mine, :] + sums_in[n].astype(F32)
                )

    s_pair, c_pair = tsum[mine, :], csum[mine, :]
    s_next = fac0 * s_pair + s0_half
    c_next = fac1 * c_pair + c1_half
    half_out[0] = jnp.where(is_first, s_next, s_pair).astype(BF16)
    half_out[1] = jnp.where(is_first, c_pair, c_next).astype(BF16)
    for n in range(2):
        to_sibling(n, half_out, half_in, half_send, half_recv).start()
    tsum[mine, :] = jnp.where(is_first, s_pair, s_next)
    csum[mine, :] = jnp.where(is_first, c_next, c_pair)
    for n, total in enumerate((tsum, csum)):
        to_sibling(n, half_out, half_in, half_send, half_recv).wait_recv()
        total[others, :] = half_in[n].astype(F32)

    skip = widen(jnp.broadcast_to(skip_ref[...], (8, skip_ref.shape[1])), width)[0:1, :]

    def one(c, flip, left_ref, right_ref, a_ref, b_ref, outer_ref, stack, carry, out, small, small_local):
        at = rows_at(c, CHUNK)
        lhs, rhs = left_ref[at, :], right_ref[at, :]
        x = a_ref[at, :]
        first, second = (factor(3, c), factor(2, c)) if flip else (factor(2, c), factor(3, c))
        mask = upper if flip else lower
        gram = lax.dot_general(lhs, rhs, NT, preferred_element_type=F32)
        gram = jnp.where(mask, gram, 0.0).astype(BF16)
        low = first * carry[...]
        stack[0:CHUNK, :] = x
        stack[CHUNK:, :] = low.astype(BF16)
        turned = rhs.astype(F32).T.astype(BF16)
        both = jnp.concatenate(
            [
                jnp.concatenate([gram, lhs], axis=1),
                jnp.concatenate([turned, jnp.zeros((turned.shape[0], lhs.shape[1]), BF16)], axis=1),
            ],
            axis=0,
        )
        result = jnp.dot(both, stack[...], preferred_element_type=F32)
        outer = widen(outer_ref[at, :], width)
        out[at, :] = (outer * (result[:CHUNK] + skip * x.astype(F32))).astype(BF16)
        carry[...] = second * (low + result[CHUNK:])
        cross = lax.dot_general(b_ref[at, :], stack[CHUNK:, :], NT, preferred_element_type=F32)
        small[at, :] = (small_local[at, :] + cross).astype(BF16)

    def rs_copy(which, k, j, c, peer):
        src = (rpart, wpart)[which]
        return pltpu.make_async_remote_copy(
            src_ref=src.at[rows_at(c, CHUNK)],
            dst_ref=got.at[which, k - 1, rows_at(j, CHUNK)],
            send_sem=rs_send.at[which, k - 1, j],
            recv_sem=rs_recv.at[which, k - 1, j],
            device_id={"tp": peer},
            device_id_type=MESH,
        )

    def send_part(which, c):
        peer = c // per
        k = lax.rem(peer - tp + ntp, ntp)

        @pl.when(k != 0)
        def _():
            rs_copy(which, k, c - peer * per, c, peer).start()

    def block(i, carry):
        j = chunks - 1 - i
        one(i, False, qbuf, kbuf, xs_ref, gs_ref, eb_ref, fstack, tsum, mixed_ref, rpart, rlocal)
        one(j, True, kbuf, qbuf, gs_ref, xs_ref, ea_ref, bstack, csum, grad_ref, wpart, wlocal)
        send_part(0, i)
        send_part(1, j)
        return carry

    lax.fori_loop(0, chunks, block, 0)

    for which, (src, out) in enumerate(((rpart, rout), (wpart, wout))):
        total = src[own, :].astype(F32)
        for k in range(1, ntp):
            for j in range(per):
                rs_copy(which, k, j, 0, lax.rem(tp + k, ntp)).wait_recv()
            total = total + got[which, k - 1].astype(F32)
        out[...] = total.astype(BF16)

    for k in range(1, ntp):
        for which in range(2):
            ag_copy(which, k, tp).wait_send()
            for j in range(per):
                peer = lax.rem(tp + k, ntp)
                rs_copy(which, k, j, peer * per + j, peer).wait_send()

    for k in range(1, nseq):
        log_copy(k, seq).wait_send()
    for n in range(2):
        to_sibling(n, pair_out, pair_in, pair_send, pair_recv).wait_send()
        to_sibling(n, half_out, half_in, half_send, half_recv).wait_send()
    for k in range(1, groups):
        sum_copy(0, k, group).wait_send()


def local(nseq, ntp, head_inputs, write_keys, read_queries, log_decay, skip_gain, out_grad):
    tokens, width = head_inputs.shape
    rows, size = write_keys.shape
    heads = log_decay.shape[0]
    chunks = tokens // CHUNK
    vmem = pl.BlockSpec(memory_space=pltpu.VMEM)
    hbm = pl.BlockSpec(memory_space=pl.ANY)
    dma = pltpu.SemaphoreType.DMA
    big = pltpu.VMEM((tokens, width), BF16)
    part = pltpu.VMEM((rows, size), BF16)
    wide, tall = pltpu.VMEM((tokens, width), BF16), pltpu.VMEM((tokens, size), BF16)
    total = pltpu.VMEM((size, width), F32)
    halves = pltpu.VMEM((2, size // 2, width), BF16)
    small = pltpu.VMEM((tokens, size), F32)
    groups = nseq // 2
    lanes = -(-heads // LANES) * LANES
    by_head = pltpu.VMEM((tokens, heads), F32)
    stack = pltpu.VMEM((CHUNK + size, width), BF16)
    return pl.pallas_call(
        functools.partial(kernel, nseq, ntp),
        out_shape=(big, big, part, part),
        in_specs=[hbm, hbm, vmem, vmem, vmem, vmem],
        out_specs=[vmem] * 4,
        scratch_shapes=[wide] * 6
        + [tall, tall, total, total, pltpu.VMEM((4 * chunks, width), F32), by_head, by_head]
        + [pltpu.VMEM((nseq, 8, lanes), F32)]
        + [pltpu.VMEM((8 * groups, width), F32), pltpu.VMEM((16, width), F32)]
        + [halves, halves, halves, pltpu.VMEM((groups, size // 2, width), BF16), halves, halves]
        + [stack, stack, tall, tall, small, small, pltpu.VMEM((2, ntp - 1, rows, size), BF16)]
        + [dma((2, chunks)), dma((2, ntp)), dma((2, ntp)), dma((nseq,)), dma((nseq,))]
        + [dma((2,)), dma((2,)), dma((groups,)), dma((groups,)), dma((2,)), dma((2,))]
        + [dma((2, ntp - 1, rows // CHUNK))] * 2,
        compiler_params=pltpu.CompilerParams(
            collective_id=0, has_side_effects=True, vmem_limit_bytes=LIMIT
        ),
        name="ssd_layer",
    )(head_inputs, out_grad, write_keys, read_queries, log_decay, skip_gain[None, :])


def solution(mesh):
    in_specs = (
        P("seq", "tp"),
        P(("seq", "tp"), None),
        P(("seq", "tp"), None),
        P("tp", "seq"),
        P("tp"),
        P("seq", "tp"),
    )
    out_specs = (P("seq", "tp"), P("seq", "tp"), P(("seq", "tp"), None), P(("seq", "tp"), None))
    body = functools.partial(local, mesh.shape["seq"], mesh.shape["tp"])
    return jax.shard_map(body, mesh=mesh, in_specs=in_specs, out_specs=out_specs, check_vma=False)
```

```python
import functools
import jax
import jax.numpy as jnp
from jax import lax
from jax.experimental import pallas as pl
from jax.experimental.pallas import tpu as pltpu
from jax.sharding import PartitionSpec as P

CHUNK = 128
HALF = CHUNK // 2
LANES = 128
MESH = pl.DeviceIdType.MESH
F32 = jnp.float32
BF16 = jnp.bfloat16
LIMIT = 56 * 1024 * 1024
NT = (((1,), (1,)), ((), ()))
TN = (((0,), (0,)), ((), ()))


def exact_nt(a, b):
    return lax.dot_general(a, b, NT, precision=lax.Precision.HIGHEST, preferred_element_type=F32)


def widen(values, width):
    rows, heads = values.shape
    dim = width // heads
    each = LANES // dim
    lane = lax.broadcasted_iota(jnp.int32, (rows, LANES), 1)
    tiles = []
    for p in range(width // LANES):
        tile = jnp.broadcast_to(values[:, p * each : p * each + 1], (rows, LANES))
        for e in range(1, each):
            h = p * each + e
            nxt = jnp.broadcast_to(values[:, h : h + 1], (rows, LANES))
            tile = jnp.where(lane >= e * dim, nxt, tile)
        tiles.append(tile)
    return jnp.concatenate(tiles, axis=1)


def rows_at(c, size):
    return pl.ds(pl.multiple_of(c * size, size), size)


def kernel(
    nseq, ntp,
    x_hbm, g_hbm, k_ref, q_ref, ld_ref, skip_ref,
    mixed_ref, grad_ref, wout, rout,
    x_ref, g_ref, xs_ref, gs_ref, xe_ref, ge_ref, kbuf, qbuf, tsum, csum, factors, ea_ref, eb_ref,
    logsum, pairfac, corefac, pair_out, pair_in, sums_out, sums_in, half_out, half_in,
    fstack, bstack, wpart, rpart, wlocal, rlocal, sadd, cadd, got,
    load_sem, ag_send, ag_recv, log_send, log_recv, pair_send, pair_recv, sum_send, sum_recv,
    half_send, half_recv, rs_send, rs_recv,
):
    seq, tp = lax.axis_index("seq"), lax.axis_index("tp")
    rows = k_ref.shape[0]
    tokens, width = x_ref.shape
    chunks = tokens // CHUNK
    per = rows // CHUNK
    groups = nseq // 2
    group = seq // 2
    core = seq - 2 * group
    sibling = 2 * group + 1 - core
    heads = ld_ref.shape[0]

    def load(which, c):
        src, dst = ((x_hbm, x_ref), (g_hbm, g_ref))[which]
        at = rows_at(c, CHUNK)
        return pltpu.make_async_copy(src.at[at], dst.at[at], load_sem.at[which, c])

    def start_loads(c, carry):
        load(0, c).start()
        load(1, c).start()
        return carry

    lax.fori_loop(0, chunks, start_loads, 0)

    barrier = pltpu.get_barrier_semaphore()
    for k in range(1, ntp):
        pl.semaphore_signal(
            barrier, inc=1, device_id={"tp": lax.rem(tp + k, ntp)}, device_id_type=MESH
        )
    for k in range(1, nseq):
        pl.semaphore_signal(
            barrier, inc=1, device_id={"seq": lax.rem(seq + k, nseq)}, device_id_type=MESH
        )
    pl.semaphore_wait(barrier, ntp - 1 + nseq - 1)

    def ag_copy(which, k, place):
        src, dst = ((k_ref, kbuf), (q_ref, qbuf))[which]
        return pltpu.make_async_remote_copy(
            src_ref=src,
            dst_ref=dst.at[rows_at(place, rows)],
            send_sem=ag_send.at[which, k],
            recv_sem=ag_recv.at[which, k],
            device_id={"tp": lax.rem(tp + k, ntp)},
            device_id_type=MESH,
        )

    for which in range(2):
        for k in range(ntp - 1, 0, -1):
            ag_copy(which, k, tp).start()

    own = rows_at(tp, rows)
    kbuf[own, :] = k_ref[...]
    qbuf[own, :] = q_ref[...]

    row = lax.broadcasted_iota(jnp.int32, (chunks, tokens), 0) * CHUNK
    col = lax.broadcasted_iota(jnp.int32, (chunks, tokens), 1)
    before = jnp.where(col < row + HALF, 1.0, 0.0)
    logs = ld_ref[...]
    kinds = (
        1.0 - before,
        before,
        jnp.where(col >= row, before, 0.0),
        jnp.where(col < row + CHUNK, 1.0 - before, 0.0),
    )
    whole_log = exact_nt(jnp.ones((8, tokens), F32), logs)
    logsum[seq] = jnp.zeros((8, logsum.shape[2]), F32)
    logsum[seq, :, 0:heads] = whole_log

    def log_copy(k, place):
        return pltpu.make_async_remote_copy(
            src_ref=logsum.at[place],
            dst_ref=logsum.at[place],
            send_sem=log_send.at[k],
            recv_sem=log_recv.at[k],
            device_id={"seq": lax.rem(seq + k, nseq)},
            device_id_type=MESH,
        )

    for k in range(1, nseq):
        log_copy(k, seq).start()
    for n, kind in enumerate(kinds):
        factors[n * chunks : (n + 1) * chunks, :] = widen(jnp.exp(exact_nt(kind, logs)), width)

    def factor(n, c):
        return factors[pl.ds(n * chunks + c, 1), :]

    trow = lax.broadcasted_iota(jnp.int32, (CHUNK, CHUNK), 0)
    tcol = lax.broadcasted_iota(jnp.int32, (CHUNK, CHUNK), 1)
    lower, upper = trow >= tcol, trow <= tcol
    about_middle = jnp.where(lower, 1.0, 0.0) - jnp.where(tcol < HALF, 1.0, 0.0)

    def scale(which, c, carry):
        src, dst, end = ((x_ref, xs_ref, xe_ref), (g_ref, gs_ref, ge_ref))[which]
        at = rows_at(c, CHUNK)
        d = exact_nt(about_middle, ld_ref[:, at])
        spread = jnp.exp(d if which else -d)
        (eb_ref if which else ea_ref)[at, :] = spread
        load(which, c).wait()
        value = src[at, :].astype(F32) * widen(spread, width)
        dst[at, :] = value.astype(BF16)
        end[at, :] = (value * factor(which, c)).astype(BF16)
        return carry

    scale_inputs, scale_grads = functools.partial(scale, 0), functools.partial(scale, 1)
    lax.fori_loop(0, chunks, scale_inputs, 0)

    for k in range(1, nseq):
        log_copy(k, lax.rem(seq - k + nseq, nseq)).wait_recv()
    for n in range(groups):
        both_logs = logsum[2 * n, :, 0:heads] + logsum[2 * n + 1, :, 0:heads]
        pairfac[8 * n : 8 * n + 8, :] = widen(jnp.exp(both_logs), width)
    for n in range(2):
        corefac[8 * n : 8 * n + 8, :] = widen(jnp.exp(logsum[2 * group + n, :, 0:heads]), width)

    half = tsum.shape[0] // 2
    mine, others = rows_at(core, half), rows_at(1 - core, half)
    fac0, fac1 = corefac[0:1, :], corefac[8:9, :]
    is_first = core == 0

    def to_sibling(n, src, dst, send, recv):
        return pltpu.make_async_remote_copy(
            src_ref=src.at[n],
            dst_ref=dst.at[n],
            send_sem=send.at[n],
            recv_sem=recv.at[n],
            device_id={"seq": sibling},
            device_id_type=MESH,
        )

    def pair_copy(n):
        return to_sibling(n, pair_out, pair_in, pair_send, pair_recv)

    def half_copy(n):
        return to_sibling(n, half_out, half_in, half_send, half_recv)

    def sum_copy(n, k, place):
        peer = lax.rem(group + k, groups)
        return pltpu.make_async_remote_copy(
            src_ref=sums_out.at[n],
            dst_ref=sums_in.at[place],
            send_sem=sum_send.at[k],
            recv_sem=sum_recv.at[place],
            device_id={"seq": 2 * peer + core},
            device_id_type=MESH,
        )

    def end_sum(which):
        buf, scaled, total = ((kbuf, xe_ref, tsum), (qbuf, ge_ref, csum))[which]
        for k in range(ntp):
            place = lax.rem(tp - k + ntp, ntp)
            if k > 0:
                ag_copy(which, k, place).wait_recv()
            at = rows_at(place, rows)
            term = lax.dot_general(buf[at, :], scaled[at, :], TN, preferred_element_type=F32)
            if k == 0:
                total[...] = term
            else:
                total[...] += term
        pair_out[which] = total[others, :].astype(BF16)
        pair_copy(which).start()

    def send_sums(which):
        total = (tsum, csum)[which]
        pair_copy(which).wait_recv()
        ours, theirs = total[mine, :], pair_in[which].astype(F32)
        zeroth, first = jnp.where(is_first, ours, theirs), jnp.where(is_first, theirs, ours)
        joined = fac0 * first + zeroth if which else fac1 * zeroth + first
        sums_out[which] = joined.astype(BF16)
        for k in range(1, groups):
            later = group + k < groups

            @pl.when(jnp.logical_not(later) if which else later)
            def _(k=k):
                sum_copy(which, k, group).start()

    def enter(which):
        total = (tsum, csum)[which]
        received = pair_in[which].astype(F32)
        own_half = total[mine, :]
        total[mine, :] = jnp.zeros((half, width), F32)
        for n in range(groups - 1, -1, -1) if which else range(groups):

            @pl.when(n > group if which else n < group)
            def _(n=n):
                sum_copy(0, 1, n).wait_recv()
                total[mine, :] = (
                    pairfac[8 * n : 8 * n + 1, :] * total[mine, :] + sums_in[n].astype(F32)
                )

        into = total[mine, :]
        if which:
            beyond = fac1 * into + jnp.where(is_first, received, own_half)
            half_out[1] = jnp.where(is_first, into, beyond).astype(BF16)
            total[mine, :] = jnp.where(is_first, beyond, into)
        else:
            beyond = fac0 * into + jnp.where(is_first, own_half, received)
            half_out[0] = jnp.where(is_first, beyond, into).astype(BF16)
            total[mine, :] = jnp.where(is_first, into, beyond)
        half_copy(which).start()

    def complete(which):
        half_copy(which).wait_recv()
        (tsum, csum)[which][others, :] = half_in[which].astype(F32)

    def local_grads(c, carry):
        at = rows_at(c, CHUNK)
        mixer = lax.dot_general(gs_ref[at, :], xs_ref[at, :], NT, preferred_element_type=F32)
        mixer = jnp.where(lower, mixer, 0.0).astype(BF16)
        rlocal[at, :] = jnp.dot(mixer, kbuf[at, :], preferred_element_type=F32)
        wlocal[at, :] = lax.dot_general(mixer, qbuf[at, :], TN, preferred_element_type=F32)
        return carry

    def updates(c, carry):
        at = rows_at(c, CHUNK)
        sadd[c] = lax.dot_general(kbuf[at, :], xs_ref[at, :], TN, preferred_element_type=F32)
        cadd[c] = lax.dot_general(qbuf[at, :], gs_ref[at, :], TN, preferred_element_type=F32)
        return carry

    middle = chunks // 2
    end_sum(0)
    lax.fori_loop(0, middle, scale_grads, 0)
    send_sums(0)
    lax.fori_loop(middle, chunks, scale_grads, 0)
    end_sum(1)
    lax.fori_loop(0, middle, local_grads, 0)
    send_sums(1)
    lax.fori_loop(middle, chunks, local_grads, 0)
    lax.fori_loop(0, chunks, updates, 0)
    enter(0)

    skip = widen(jnp.broadcast_to(skip_ref[...], (8, skip_ref.shape[1])), width)[0:1, :]

    def one(c, flip, left_ref, right_ref, a_ref, b_ref, outer_ref, stack, carry, add, out, small, small_local):
        at = rows_at(c, CHUNK)
        lhs, rhs = left_ref[at, :], right_ref[at, :]
        x = a_ref[at, :]
        first, second = (factor(3, c), factor(2, c)) if flip else (factor(2, c), factor(3, c))
        mask = upper if flip else lower
        gram = lax.dot_general(lhs, rhs, NT, preferred_element_type=F32)
        gram = jnp.where(mask, gram, 0.0).astype(BF16)
        low = first * carry[...]
        stack[0:CHUNK, :] = x
        stack[CHUNK:, :] = low.astype(BF16)
        total = jnp.dot(
            jnp.concatenate([gram, lhs], axis=1), stack[...], preferred_element_type=F32
        )
        outer = widen(outer_ref[at, :], width)
        out[at, :] = (outer * (total + skip * x.astype(F32))).astype(BF16)
        carry[...] = second * (low + add[c])
        cross = lax.dot_general(b_ref[at, :], stack[CHUNK:, :], NT, preferred_element_type=F32)
        small[at, :] = (small_local[at, :] + cross).astype(BF16)

    def rs_copy(which, k, j, c, peer):
        src = (rpart, wpart)[which]
        return pltpu.make_async_remote_copy(
            src_ref=src.at[rows_at(c, CHUNK)],
            dst_ref=got.at[which, k - 1, rows_at(j, CHUNK)],
            send_sem=rs_send.at[which, k - 1, j],
            recv_sem=rs_recv.at[which, k - 1, j],
            device_id={"tp": peer},
            device_id_type=MESH,
        )

    def send_part(which, c):
        peer = c // per
        k = lax.rem(peer - tp + ntp, ntp)

        @pl.when(k != 0)
        def _():
            rs_copy(which, k, c - peer * per, c, peer).start()

    def forward(c, carry):
        one(c, False, qbuf, kbuf, xs_ref, gs_ref, eb_ref, fstack, tsum, sadd, mixed_ref, rpart, rlocal)
        send_part(0, c)
        return carry

    def backward(i, carry):
        c = chunks - 1 - i
        one(c, True, kbuf, qbuf, gs_ref, xs_ref, ea_ref, bstack, csum, cadd, grad_ref, wpart, wlocal)
        send_part(1, c)
        return carry

    late = chunks - chunks // 4
    complete(0)
    lax.fori_loop(0, late, forward, 0)
    enter(1)
    lax.fori_loop(late, chunks, forward, 0)
    complete(1)
    lax.fori_loop(0, chunks, backward, 0)

    for which, (src, out) in enumerate(((rpart, rout), (wpart, wout))):
        total = src[own, :].astype(F32)
        for k in range(1, ntp):
            for j in range(per):
                rs_copy(which, k, j, 0, lax.rem(tp + k, ntp)).wait_recv()
            total = total + got[which, k - 1].astype(F32)
        out[...] = total.astype(BF16)

    for k in range(1, ntp):
        for which in range(2):
            ag_copy(which, k, tp).wait_send()
            for j in range(per):
                peer = lax.rem(tp + k, ntp)
                rs_copy(which, k, j, peer * per + j, peer).wait_send()

    for k in range(1, nseq):
        log_copy(k, seq).wait_send()
    for n in range(2):
        pair_copy(n).wait_send()
        half_copy(n).wait_send()
    for k in range(1, groups):
        sum_copy(0, k, group).wait_send()


def store_kernel(*refs):
    sems = refs[-1]
    copies = [pltpu.make_async_copy(refs[n], refs[4 + n], sems.at[n]) for n in range(4)]
    for copy in copies:
        copy.start()
    for copy in copies:
        copy.wait()


def local(nseq, ntp, head_inputs, write_keys, read_queries, log_decay, skip_gain, out_grad):
    tokens, width = head_inputs.shape
    rows, size = write_keys.shape
    heads = log_decay.shape[0]
    chunks = tokens // CHUNK
    vmem = pl.BlockSpec(memory_space=pltpu.VMEM)
    hbm = pl.BlockSpec(memory_space=pl.ANY)
    dma = pltpu.SemaphoreType.DMA
    big = pltpu.VMEM((tokens, width), BF16)
    part = pltpu.VMEM((rows, size), BF16)
    wide, tall = pltpu.VMEM((tokens, width), BF16), pltpu.VMEM((tokens, size), BF16)
    total = pltpu.VMEM((size, width), F32)
    halves = pltpu.VMEM((2, size // 2, width), BF16)
    small = pltpu.VMEM((tokens, size), F32)
    adds = pltpu.VMEM((chunks, size, width), F32)
    groups = nseq // 2
    lanes = -(-heads // LANES) * LANES
    by_head = pltpu.VMEM((tokens, heads), F32)
    stack = pltpu.VMEM((CHUNK + size, width), BF16)
    results = pl.pallas_call(
        functools.partial(kernel, nseq, ntp),
        out_shape=(big, big, part, part),
        in_specs=[hbm, hbm, vmem, vmem, vmem, vmem],
        out_specs=[vmem] * 4,
        scratch_shapes=[wide] * 6
        + [tall, tall, total, total, pltpu.VMEM((4 * chunks, width), F32), by_head, by_head]
        + [pltpu.VMEM((nseq, 8, lanes), F32)]
        + [pltpu.VMEM((8 * groups, width), F32), pltpu.VMEM((16, width), F32)]
        + [halves, halves, halves, pltpu.VMEM((groups, size // 2, width), BF16), halves, halves]
        + [stack, stack, tall, tall, small, small, adds, adds, pltpu.VMEM((2, ntp - 1, rows, size), BF16)]
        + [dma((2, chunks)), dma((2, ntp)), dma((2, ntp)), dma((nseq,)), dma((nseq,))]
        + [dma((2,)), dma((2,)), dma((groups,)), dma((groups,)), dma((2,)), dma((2,))]
        + [dma((2, ntp - 1, rows // CHUNK))] * 2,
        compiler_params=pltpu.CompilerParams(
            collective_id=0, has_side_effects=True, vmem_limit_bytes=LIMIT
        ),
        name="ssd_layer",
    )(head_inputs, out_grad, write_keys, read_queries, log_decay, skip_gain[None, :])
    return pl.pallas_call(
        store_kernel,
        out_shape=tuple(jax.ShapeDtypeStruct(r.shape, r.dtype) for r in results),
        in_specs=[vmem] * 4,
        out_specs=[hbm] * 4,
        scratch_shapes=[dma((4,))],
        name="store_results",
    )(*results)


def solution(mesh):
    in_specs = (
        P("seq", "tp"),
        P(("seq", "tp"), None),
        P(("seq", "tp"), None),
        P("tp", "seq"),
        P("tp"),
        P("seq", "tp"),
    )
    out_specs = (P("seq", "tp"), P("seq", "tp"), P(("seq", "tp"), None), P(("seq", "tp"), None))
    body = functools.partial(local, mesh.shape["seq"], mesh.shape["tp"])
    return jax.shard_map(body, mesh=mesh, in_specs=in_specs, out_specs=out_specs, check_vma=False)
```

```python
import functools
import jax
import jax.numpy as jnp
from jax import lax
from jax.experimental import pallas as pl
from jax.experimental.pallas import tpu as pltpu
from jax.sharding import PartitionSpec as P

CHUNK = 128
HALF = CHUNK // 2
LANES = 128
MESH = pl.DeviceIdType.MESH
F32 = jnp.float32
BF16 = jnp.bfloat16
LIMIT = 56 * 1024 * 1024
NT = (((1,), (1,)), ((), ()))
TN = (((0,), (0,)), ((), ()))


def exact_nt(a, b):
    return lax.dot_general(a, b, NT, precision=lax.Precision.HIGHEST, preferred_element_type=F32)


def widen(values, width):
    rows, heads = values.shape
    dim = width // heads
    each = LANES // dim
    lane = lax.broadcasted_iota(jnp.int32, (rows, LANES), 1)
    tiles = []
    for p in range(width // LANES):
        tile = jnp.broadcast_to(values[:, p * each : p * each + 1], (rows, LANES))
        for e in range(1, each):
            h = p * each + e
            nxt = jnp.broadcast_to(values[:, h : h + 1], (rows, LANES))
            tile = jnp.where(lane >= e * dim, nxt, tile)
        tiles.append(tile)
    return jnp.concatenate(tiles, axis=1)


def rows_at(c, size):
    return pl.ds(pl.multiple_of(c * size, size), size)


def kernel(
    nseq, ntp,
    x_hbm, g_hbm, k_ref, q_ref, ld_ref, skip_ref,
    mixed_ref, grad_ref, wout, rout,
    xs_ref, gs_ref, xe_ref, ge_ref, kbuf, qbuf, tsum, csum, factors, ea_ref, eb_ref,
    logsum, pairfac, corefac, pair_out, pair_in, sums_out, sums_in, half_out, half_in,
    fstack0, bstack0, fstack1, bstack1, wpart, rpart, wlocal, rlocal, sadd, cadd, got,
    load_sem, ag_send, ag_recv, log_send, log_recv, pair_send, pair_recv, sum_send, sum_recv,
    half_send, half_recv, rs_send, rs_recv,
):
    seq, tp = lax.axis_index("seq"), lax.axis_index("tp")
    rows = k_ref.shape[0]
    tokens, width = xs_ref.shape
    chunks = tokens // CHUNK
    per = rows // CHUNK
    groups = nseq // 2
    group = seq // 2
    core = seq - 2 * group
    sibling = 2 * group + 1 - core
    heads = ld_ref.shape[0]

    def load(which, c):
        src, dst = ((x_hbm, xe_ref), (g_hbm, ge_ref))[which]
        at = rows_at(c, CHUNK)
        return pltpu.make_async_copy(src.at[at], dst.at[at], load_sem.at[which, c])

    def start_loads(c, carry):
        load(0, c).start()
        load(1, c).start()
        return carry

    lax.fori_loop(0, chunks, start_loads, 0)

    barrier = pltpu.get_barrier_semaphore()
    for k in range(1, ntp):
        pl.semaphore_signal(
            barrier, inc=1, device_id={"tp": lax.rem(tp + k, ntp)}, device_id_type=MESH
        )
    for k in range(1, nseq):
        pl.semaphore_signal(
            barrier, inc=1, device_id={"seq": lax.rem(seq + k, nseq)}, device_id_type=MESH
        )
    pl.semaphore_wait(barrier, ntp - 1 + nseq - 1)

    def ag_copy(which, k, place):
        src, dst = ((k_ref, kbuf), (q_ref, qbuf))[which]
        return pltpu.make_async_remote_copy(
            src_ref=src,
            dst_ref=dst.at[rows_at(place, rows)],
            send_sem=ag_send.at[which, k],
            recv_sem=ag_recv.at[which, k],
            device_id={"tp": lax.rem(tp + k, ntp)},
            device_id_type=MESH,
        )

    for which in range(2):
        for k in range(ntp - 1, 0, -1):
            ag_copy(which, k, tp).start()

    own = rows_at(tp, rows)
    kbuf[own, :] = k_ref[...]
    qbuf[own, :] = q_ref[...]

    row = lax.broadcasted_iota(jnp.int32, (chunks, tokens), 0) * CHUNK
    col = lax.broadcasted_iota(jnp.int32, (chunks, tokens), 1)
    before = jnp.where(col < row + HALF, 1.0, 0.0)
    logs = ld_ref[...]
    kinds = (
        1.0 - before,
        before,
        jnp.where(col >= row, before, 0.0),
        jnp.where(col < row + CHUNK, 1.0 - before, 0.0),
    )
    whole_log = exact_nt(jnp.ones((8, tokens), F32), logs)
    logsum[seq] = jnp.zeros((8, logsum.shape[2]), F32)
    logsum[seq, :, 0:heads] = whole_log

    def log_copy(k, place):
        return pltpu.make_async_remote_copy(
            src_ref=logsum.at[place],
            dst_ref=logsum.at[place],
            send_sem=log_send.at[k],
            recv_sem=log_recv.at[k],
            device_id={"seq": lax.rem(seq + k, nseq)},
            device_id_type=MESH,
        )

    for k in range(1, nseq):
        log_copy(k, seq).start()
    for n, kind in enumerate(kinds):
        factors[n * chunks : (n + 1) * chunks, :] = widen(jnp.exp(exact_nt(kind, logs)), width)

    def factor(n, c):
        return factors[pl.ds(n * chunks + c, 1), :]

    trow = lax.broadcasted_iota(jnp.int32, (CHUNK, CHUNK), 0)
    tcol = lax.broadcasted_iota(jnp.int32, (CHUNK, CHUNK), 1)
    lower, upper = trow >= tcol, trow <= tcol
    about_middle = jnp.where(lower, 1.0, 0.0) - jnp.where(tcol < HALF, 1.0, 0.0)

    def scale(which, c, carry):
        dst, end = ((xs_ref, xe_ref), (gs_ref, ge_ref))[which]
        at = rows_at(c, CHUNK)
        d = exact_nt(about_middle, ld_ref[:, at])
        spread = widen(jnp.exp(d if which else -d), width)
        (eb_ref if which else ea_ref)[at, :] = spread
        load(which, c).wait()
        value = end[at, :].astype(F32) * spread
        dst[at, :] = value.astype(BF16)
        end[at, :] = (value * factor(which, c)).astype(BF16)
        return carry

    scale_inputs, scale_grads = functools.partial(scale, 0), functools.partial(scale, 1)
    lax.fori_loop(0, chunks, scale_inputs, 0)

    for k in range(1, nseq):
        log_copy(k, lax.rem(seq - k + nseq, nseq)).wait_recv()
    for n in range(groups):
        both_logs = logsum[2 * n, :, 0:heads] + logsum[2 * n + 1, :, 0:heads]
        pairfac[8 * n : 8 * n + 8, :] = widen(jnp.exp(both_logs), width)
    for n in range(2):
        corefac[8 * n : 8 * n + 8, :] = widen(jnp.exp(logsum[2 * group + n, :, 0:heads]), width)

    half = tsum.shape[0] // 2
    mine, others = rows_at(core, half), rows_at(1 - core, half)
    fac0, fac1 = corefac[0:1, :], corefac[8:9, :]
    is_first = core == 0

    def to_sibling(n, src, dst, send, recv):
        return pltpu.make_async_remote_copy(
            src_ref=src.at[n],
            dst_ref=dst.at[n],
            send_sem=send.at[n],
            recv_sem=recv.at[n],
            device_id={"seq": sibling},
            device_id_type=MESH,
        )

    def pair_copy(n):
        return to_sibling(n, pair_out, pair_in, pair_send, pair_recv)

    def half_copy(n):
        return to_sibling(n, half_out, half_in, half_send, half_recv)

    def sum_copy(n, k, place):
        peer = lax.rem(group + k, groups)
        return pltpu.make_async_remote_copy(
            src_ref=sums_out.at[n],
            dst_ref=sums_in.at[place],
            send_sem=sum_send.at[k],
            recv_sem=sum_recv.at[place],
            device_id={"seq": 2 * peer + core},
            device_id_type=MESH,
        )

    def end_sum(which):
        buf, scaled, total = ((kbuf, xe_ref, tsum), (qbuf, ge_ref, csum))[which]
        for k in range(ntp):
            place = lax.rem(tp - k + ntp, ntp)
            if k > 0:
                ag_copy(which, k, place).wait_recv()
            at = rows_at(place, rows)
            term = lax.dot_general(buf[at, :], scaled[at, :], TN, preferred_element_type=F32)
            if k == 0:
                total[...] = term
            else:
                total[...] += term
        pair_out[which] = total[others, :].astype(BF16)
        pair_copy(which).start()

    def send_sums(which):
        total = (tsum, csum)[which]
        pair_copy(which).wait_recv()
        ours, theirs = total[mine, :], pair_in[which].astype(F32)
        zeroth, first = jnp.where(is_first, ours, theirs), jnp.where(is_first, theirs, ours)
        joined = fac0 * first + zeroth if which else fac1 * zeroth + first
        sums_out[which] = joined.astype(BF16)
        for k in range(1, groups):
            later = group + k < groups

            @pl.when(jnp.logical_not(later) if which else later)
            def _(k=k):
                sum_copy(which, k, group).start()

    def enter(which):
        total = (tsum, csum)[which]
        received = pair_in[which].astype(F32)
        own_half = total[mine, :]
        total[mine, :] = jnp.zeros((half, width), F32)
        for n in range(groups - 1, -1, -1) if which else range(groups):

            @pl.when(n > group if which else n < group)
            def _(n=n):
                sum_copy(0, 1, n).wait_recv()
                total[mine, :] = (
                    pairfac[8 * n : 8 * n + 1, :] * total[mine, :] + sums_in[n].astype(F32)
                )

        into = total[mine, :]
        if which:
            beyond = fac1 * into + jnp.where(is_first, received, own_half)
            half_out[1] = jnp.where(is_first, into, beyond).astype(BF16)
            total[mine, :] = jnp.where(is_first, beyond, into)
        else:
            beyond = fac0 * into + jnp.where(is_first, own_half, received)
            half_out[0] = jnp.where(is_first, beyond, into).astype(BF16)
            total[mine, :] = jnp.where(is_first, into, beyond)
        half_copy(which).start()

    def complete(which):
        half_copy(which).wait_recv()
        (tsum, csum)[which][others, :] = half_in[which].astype(F32)

    def local_grads(c, carry):
        at = rows_at(c, CHUNK)
        mixer = lax.dot_general(gs_ref[at, :], xs_ref[at, :], NT, preferred_element_type=F32)
        mixer = jnp.where(lower, mixer, 0.0).astype(BF16)
        rlocal[at, :] = jnp.dot(mixer, kbuf[at, :], preferred_element_type=F32)
        wlocal[at, :] = lax.dot_general(mixer, qbuf[at, :], TN, preferred_element_type=F32)
        return carry

    def updates(c, carry):
        at = rows_at(c, CHUNK)
        sadd[c] = lax.dot_general(kbuf[at, :], xs_ref[at, :], TN, preferred_element_type=F32)
        cadd[c] = lax.dot_general(qbuf[at, :], gs_ref[at, :], TN, preferred_element_type=F32)
        return carry

    middle = chunks // 2
    end_sum(0)
    lax.fori_loop(0, middle, scale_grads, 0)
    send_sums(0)
    lax.fori_loop(middle, chunks, scale_grads, 0)
    end_sum(1)
    lax.fori_loop(0, middle, local_grads, 0)
    send_sums(1)
    lax.fori_loop(middle, chunks, local_grads, 0)
    lax.fori_loop(0, chunks, updates, 0)
    enter(0)

    skip = widen(jnp.broadcast_to(skip_ref[...], (8, skip_ref.shape[1])), width)[0:1, :]

    def one(c, flip, left_ref, right_ref, a_ref, b_ref, outer_ref, stack, carry, add, out, small, small_local):
        at = rows_at(c, CHUNK)
        lhs, rhs = left_ref[at, :], right_ref[at, :]
        x = a_ref[at, :]
        first, second = (factor(3, c), factor(2, c)) if flip else (factor(2, c), factor(3, c))
        mask = upper if flip else lower
        gram = lax.dot_general(lhs, rhs, NT, preferred_element_type=F32)
        gram = jnp.where(mask, gram, 0.0).astype(BF16)
        low = first * carry[...]
        stack[0:CHUNK, :] = x
        stack[CHUNK:, :] = low.astype(BF16)
        total = jnp.dot(
            jnp.concatenate([gram, lhs], axis=1), stack[...], preferred_element_type=F32
        )
        out[at, :] = (outer_ref[at, :] * (total + skip * x.astype(F32))).astype(BF16)
        carry[...] = second * (low + add[c])
        cross = lax.dot_general(b_ref[at, :], stack[CHUNK:, :], NT, preferred_element_type=F32)
        small[at, :] = (small_local[at, :] + cross).astype(BF16)

    def rs_copy(which, k, j, c, peer):
        src = (rpart, wpart)[which]
        return pltpu.make_async_remote_copy(
            src_ref=src.at[rows_at(c, CHUNK)],
            dst_ref=got.at[which, k - 1, rows_at(j, CHUNK)],
            send_sem=rs_send.at[which, k - 1, j],
            recv_sem=rs_recv.at[which, k - 1, j],
            device_id={"tp": peer},
            device_id_type=MESH,
        )

    def send_part(which, c):
        peer = c // per
        k = lax.rem(peer - tp + ntp, ntp)

        @pl.when(k != 0)
        def _():
            rs_copy(which, k, c - peer * per, c, peer).start()

    def forward(c, stack):
        one(c, False, qbuf, kbuf, xs_ref, gs_ref, eb_ref, stack, tsum, sadd, mixed_ref, rpart, rlocal)

    def backward(c, stack):
        one(c, True, kbuf, qbuf, gs_ref, xs_ref, ea_ref, stack, csum, cadd, grad_ref, wpart, wlocal)

    def two_blocks(m, carry):
        i, j = 2 * m, chunks - 1 - 2 * m
        forward(i, fstack0)
        backward(j, bstack0)
        forward(i + 1, fstack1)
        backward(j - 1, bstack1)
        send_part(0, i)
        send_part(1, j)
        send_part(0, i + 1)
        send_part(1, j - 1)
        return carry

    enter(1)
    complete(0)
    complete(1)
    lax.fori_loop(0, chunks // 2, two_blocks, 0)

    for which, (src, out) in enumerate(((rpart, rout), (wpart, wout))):
        total = src[own, :].astype(F32)
        for k in range(1, ntp):
            for j in range(per):
                rs_copy(which, k, j, 0, lax.rem(tp + k, ntp)).wait_recv()
            total = total + got[which, k - 1].astype(F32)
        out[...] = total.astype(BF16)

    for k in range(1, ntp):
        for which in range(2):
            ag_copy(which, k, tp).wait_send()
            for j in range(per):
                peer = lax.rem(tp + k, ntp)
                rs_copy(which, k, j, peer * per + j, peer).wait_send()

    for k in range(1, nseq):
        log_copy(k, seq).wait_send()
    for n in range(2):
        pair_copy(n).wait_send()
        half_copy(n).wait_send()
    for k in range(1, groups):
        sum_copy(0, k, group).wait_send()


def local(nseq, ntp, head_inputs, write_keys, read_queries, log_decay, skip_gain, out_grad):
    tokens, width = head_inputs.shape
    rows, size = write_keys.shape
    heads = log_decay.shape[0]
    chunks = tokens // CHUNK
    vmem = pl.BlockSpec(memory_space=pltpu.VMEM)
    hbm = pl.BlockSpec(memory_space=pl.ANY)
    dma = pltpu.SemaphoreType.DMA
    big = pltpu.VMEM((tokens, width), BF16)
    part = pltpu.VMEM((rows, size), BF16)
    wide, tall = pltpu.VMEM((tokens, width), BF16), pltpu.VMEM((tokens, size), BF16)
    total = pltpu.VMEM((size, width), F32)
    halves = pltpu.VMEM((2, size // 2, width), BF16)
    small = pltpu.VMEM((tokens, size), F32)
    adds = pltpu.VMEM((chunks, size, width), F32)
    groups = nseq // 2
    lanes = -(-heads // LANES) * LANES
    outer = pltpu.VMEM((tokens, width), F32)
    stack = pltpu.VMEM((CHUNK + size, width), BF16)
    return pl.pallas_call(
        functools.partial(kernel, nseq, ntp),
        out_shape=(big, big, part, part),
        in_specs=[hbm, hbm, vmem, vmem, vmem, vmem],
        out_specs=[vmem] * 4,
        scratch_shapes=[wide] * 4
        + [tall, tall, total, total, pltpu.VMEM((4 * chunks, width), F32), outer, outer]
        + [pltpu.VMEM((nseq, 8, lanes), F32)]
        + [pltpu.VMEM((8 * groups, width), F32), pltpu.VMEM((16, width), F32)]
        + [halves, halves, halves, pltpu.VMEM((groups, size // 2, width), BF16), halves, halves]
        + [stack] * 4
        + [tall, tall, small, small, adds, adds, pltpu.VMEM((2, ntp - 1, rows, size), BF16)]
        + [dma((2, chunks)), dma((2, ntp)), dma((2, ntp)), dma((nseq,)), dma((nseq,))]
        + [dma((2,)), dma((2,)), dma((groups,)), dma((groups,)), dma((2,)), dma((2,))]
        + [dma((2, ntp - 1, rows // CHUNK))] * 2,
        compiler_params=pltpu.CompilerParams(
            collective_id=0, has_side_effects=True, vmem_limit_bytes=LIMIT
        ),
        name="ssd_layer",
    )(head_inputs, out_grad, write_keys, read_queries, log_decay, skip_gain[None, :])


def solution(mesh):
    in_specs = (
        P("seq", "tp"),
        P(("seq", "tp"), None),
        P(("seq", "tp"), None),
        P("tp", "seq"),
        P("tp"),
        P("seq", "tp"),
    )
    out_specs = (P("seq", "tp"), P("seq", "tp"), P(("seq", "tp"), None), P(("seq", "tp"), None))
    body = functools.partial(local, mesh.shape["seq"], mesh.shape["tp"])
    return jax.shard_map(body, mesh=mesh, in_specs=in_specs, out_specs=out_specs, check_vma=False)
```

```python
import functools
import jax
import jax.numpy as jnp
from jax import lax
from jax.experimental import pallas as pl
from jax.experimental.pallas import tpu as pltpu
from jax.sharding import PartitionSpec as P

CHUNK = 128
HALF = CHUNK // 2
LANES = 128
MESH = pl.DeviceIdType.MESH
F32 = jnp.float32
BF16 = jnp.bfloat16
LIMIT = 56 * 1024 * 1024
NT = (((1,), (1,)), ((), ()))
TN = (((0,), (0,)), ((), ()))


def exact_nt(a, b):
    return lax.dot_general(a, b, NT, precision=lax.Precision.HIGHEST, preferred_element_type=F32)


def widen(values, width):
    rows, heads = values.shape
    dim = width // heads
    each = LANES // dim
    lane = lax.broadcasted_iota(jnp.int32, (rows, LANES), 1)
    tiles = []
    for p in range(width // LANES):
        tile = jnp.broadcast_to(values[:, p * each : p * each + 1], (rows, LANES))
        for e in range(1, each):
            h = p * each + e
            nxt = jnp.broadcast_to(values[:, h : h + 1], (rows, LANES))
            tile = jnp.where(lane >= e * dim, nxt, tile)
        tiles.append(tile)
    return jnp.concatenate(tiles, axis=1)


def rows_at(c, size):
    return pl.ds(pl.multiple_of(c * size, size), size)


def kernel(
    nseq, ntp,
    x_hbm, g_hbm, k_ref, q_ref, ld_ref, skip_ref,
    mixed_ref, grad_ref, wout, rout,
    x_ref, g_ref, xs_ref, gs_ref, xe_ref, ge_ref, kbuf, qbuf, tsum, csum, factors, ea_ref, eb_ref,
    logsum, pairfac, corefac, pair_out, pair_in, sums_out, sums_in, half_out, half_in,
    fstack0, bstack0, fstack1, bstack1, wpart, rpart, wlocal, rlocal, got,
    load_sem, ag_send, ag_recv, log_send, log_recv, pair_send, pair_recv, sum_send, sum_recv,
    half_send, half_recv, rs_send, rs_recv,
):
    seq, tp = lax.axis_index("seq"), lax.axis_index("tp")
    rows = k_ref.shape[0]
    tokens, width = x_ref.shape
    chunks = tokens // CHUNK
    per = rows // CHUNK
    groups = nseq // 2
    group = seq // 2
    core = seq - 2 * group
    sibling = 2 * group + 1 - core
    heads = ld_ref.shape[0]

    def load(which, c):
        src, dst = ((x_hbm, x_ref), (g_hbm, g_ref))[which]
        at = rows_at(c, CHUNK)
        return pltpu.make_async_copy(src.at[at], dst.at[at], load_sem.at[which, c])

    def start_loads(c, carry):
        load(0, c).start()
        load(1, c).start()
        return carry

    lax.fori_loop(0, chunks, start_loads, 0)

    barrier = pltpu.get_barrier_semaphore()
    for k in range(1, ntp):
        pl.semaphore_signal(
            barrier, inc=1, device_id={"tp": lax.rem(tp + k, ntp)}, device_id_type=MESH
        )
    for k in range(1, nseq):
        pl.semaphore_signal(
            barrier, inc=1, device_id={"seq": lax.rem(seq + k, nseq)}, device_id_type=MESH
        )
    pl.semaphore_wait(barrier, ntp - 1 + nseq - 1)

    def ag_copy(which, k, place):
        src, dst = ((k_ref, kbuf), (q_ref, qbuf))[which]
        return pltpu.make_async_remote_copy(
            src_ref=src,
            dst_ref=dst.at[rows_at(place, rows)],
            send_sem=ag_send.at[which, k],
            recv_sem=ag_recv.at[which, k],
            device_id={"tp": lax.rem(tp + k, ntp)},
            device_id_type=MESH,
        )

    for k in range(ntp - 1, 0, -1):
        for which in range(2):
            ag_copy(which, k, tp).start()

    own = rows_at(tp, rows)
    kbuf[own, :] = k_ref[...]
    qbuf[own, :] = q_ref[...]

    row = lax.broadcasted_iota(jnp.int32, (chunks, tokens), 0) * CHUNK
    col = lax.broadcasted_iota(jnp.int32, (chunks, tokens), 1)
    before = jnp.where(col < row + HALF, 1.0, 0.0)
    logs = ld_ref[...]
    kinds = (
        1.0 - before,
        before,
        jnp.where(col >= row, before, 0.0),
        jnp.where(col < row + CHUNK, 1.0 - before, 0.0),
    )
    whole_log = exact_nt(jnp.ones((8, tokens), F32), logs)
    logsum[seq] = jnp.zeros((8, logsum.shape[2]), F32)
    logsum[seq, :, 0:heads] = whole_log

    def log_copy(k, place):
        return pltpu.make_async_remote_copy(
            src_ref=logsum.at[place],
            dst_ref=logsum.at[place],
            send_sem=log_send.at[k],
            recv_sem=log_recv.at[k],
            device_id={"seq": lax.rem(seq + k, nseq)},
            device_id_type=MESH,
        )

    for k in range(1, nseq):
        log_copy(k, seq).start()
    for n, kind in enumerate(kinds):
        factors[n * chunks : (n + 1) * chunks, :] = widen(jnp.exp(exact_nt(kind, logs)), width)

    def factor(n, c):
        return factors[pl.ds(n * chunks + c, 1), :]

    trow = lax.broadcasted_iota(jnp.int32, (CHUNK, CHUNK), 0)
    tcol = lax.broadcasted_iota(jnp.int32, (CHUNK, CHUNK), 1)
    lower, upper = trow >= tcol, trow <= tcol
    about_middle = jnp.where(lower, 1.0, 0.0) - jnp.where(tcol < HALF, 1.0, 0.0)

    def scale(c, carry):
        at = rows_at(c, CHUNK)
        d = exact_nt(about_middle, ld_ref[:, at])
        a, b = widen(jnp.exp(-d), width), widen(jnp.exp(d), width)
        ea_ref[at, :] = a
        eb_ref[at, :] = b
        load(0, c).wait()
        x = x_ref[at, :].astype(F32) * a
        xs_ref[at, :] = x.astype(BF16)
        xe_ref[at, :] = (x * factor(0, c)).astype(BF16)
        load(1, c).wait()
        g = g_ref[at, :].astype(F32) * b
        gs_ref[at, :] = g.astype(BF16)
        ge_ref[at, :] = (g * factor(1, c)).astype(BF16)
        return carry

    lax.fori_loop(0, chunks, scale, 0)

    for k in range(1, nseq):
        log_copy(k, lax.rem(seq - k + nseq, nseq)).wait_recv()
    for n in range(groups):
        both_logs = logsum[2 * n, :, 0:heads] + logsum[2 * n + 1, :, 0:heads]
        pairfac[8 * n : 8 * n + 8, :] = widen(jnp.exp(both_logs), width)
    for n in range(2):
        corefac[8 * n : 8 * n + 8, :] = widen(jnp.exp(logsum[2 * group + n, :, 0:heads]), width)

    for k in range(ntp):
        place = lax.rem(tp - k + ntp, ntp)
        if k > 0:
            for which in range(2):
                ag_copy(which, k, place).wait_recv()
        at = rows_at(place, rows)
        up = lax.dot_general(kbuf[at, :], xe_ref[at, :], TN, preferred_element_type=F32)
        down = lax.dot_general(qbuf[at, :], ge_ref[at, :], TN, preferred_element_type=F32)
        if k == 0:
            tsum[...] = up
            csum[...] = down
        else:
            tsum[...] += up
            csum[...] += down

    half = tsum.shape[0] // 2
    mine, others = rows_at(core, half), rows_at(1 - core, half)

    def to_sibling(n, src, dst, send, recv):
        return pltpu.make_async_remote_copy(
            src_ref=src.at[n],
            dst_ref=dst.at[n],
            send_sem=send.at[n],
            recv_sem=recv.at[n],
            device_id={"seq": sibling},
            device_id_type=MESH,
        )

    for n, total in enumerate((tsum, csum)):
        pair_out[n] = total[others, :].astype(BF16)
        to_sibling(n, pair_out, pair_in, pair_send, pair_recv).start()
    for n in range(2):
        to_sibling(n, pair_out, pair_in, pair_send, pair_recv).wait_recv()

    fac0, fac1 = corefac[0:1, :], corefac[8:9, :]
    is_first = core == 0

    def ordered(n, total):
        ours, theirs = total[mine, :], pair_in[n].astype(F32)
        return jnp.where(is_first, ours, theirs), jnp.where(is_first, theirs, ours)

    s0, s1 = ordered(0, tsum)
    sums_out[0] = (fac1 * s0 + s1).astype(BF16)
    c0, c1 = ordered(1, csum)
    sums_out[1] = (fac0 * c1 + c0).astype(BF16)

    def sum_copy(n, k, place):
        peer = lax.rem(group + k, groups)
        return pltpu.make_async_remote_copy(
            src_ref=sums_out.at[n],
            dst_ref=sums_in.at[place],
            send_sem=sum_send.at[k],
            recv_sem=sum_recv.at[place],
            device_id={"seq": 2 * peer + core},
            device_id_type=MESH,
        )

    for k in range(1, groups):
        later = group + k < groups

        @pl.when(later)
        def _(k=k):
            sum_copy(0, k, group).start()

        @pl.when(jnp.logical_not(later))
        def _(k=k):
            sum_copy(1, k, group).start()

    def local_grads(c, carry):
        at = rows_at(c, CHUNK)
        mixer = lax.dot_general(gs_ref[at, :], xs_ref[at, :], NT, preferred_element_type=F32)
        mixer = jnp.where(lower, mixer, 0.0).astype(BF16)
        rlocal[at, :] = jnp.dot(mixer, kbuf[at, :], preferred_element_type=F32)
        wlocal[at, :] = lax.dot_general(mixer, qbuf[at, :], TN, preferred_element_type=F32)
        return carry

    lax.fori_loop(0, chunks, local_grads, 0)

    c1_half = jnp.where(is_first, pair_in[1].astype(F32), csum[mine, :])
    s0_half = jnp.where(is_first, tsum[mine, :], pair_in[0].astype(F32))
    csum[mine, :] = jnp.zeros((half, width), F32)
    tsum[mine, :] = jnp.zeros((half, width), F32)
    for order, total, test in (
        (range(groups), tsum, lambda n: n < group),
        (range(groups - 1, -1, -1), csum, lambda n: n > group),
    ):
        for n in order:

            @pl.when(test(n))
            def _(n=n, total=total):
                sum_copy(0, 1, n).wait_recv()
                total[mine, :] = (
                    pairfac[8 * n : 8 * n + 1, :] * total[mine, :] + sums_in[n].astype(F32)
                )

    s_pair, c_pair = tsum[mine, :], csum[mine, :]
    s_next = fac0 * s_pair + s0_half
    c_next = fac1 * c_pair + c1_half
    half_out[0] = jnp.where(is_first, s_next, s_pair).astype(BF16)
    half_out[1] = jnp.where(is_first, c_pair, c_next).astype(BF16)
    for n in range(2):
        to_sibling(n, half_out, half_in, half_send, half_recv).start()
    tsum[mine, :] = jnp.where(is_first, s_pair, s_next)
    csum[mine, :] = jnp.where(is_first, c_next, c_pair)
    for n, total in enumerate((tsum, csum)):
        to_sibling(n, half_out, half_in, half_send, half_recv).wait_recv()
        total[others, :] = half_in[n].astype(F32)

    skip = widen(jnp.broadcast_to(skip_ref[...], (8, skip_ref.shape[1])), width)[0:1, :]

    def one(c, flip, left_ref, right_ref, a_ref, b_ref, outer_ref, stack, carry, out, small, small_local):
        at = rows_at(c, CHUNK)
        lhs, rhs = left_ref[at, :], right_ref[at, :]
        x = a_ref[at, :]
        first, second = (factor(3, c), factor(2, c)) if flip else (factor(2, c), factor(3, c))
        mask = upper if flip else lower
        gram = lax.dot_general(lhs, rhs, NT, preferred_element_type=F32)
        gram = jnp.where(mask, gram, 0.0).astype(BF16)
        low = first * carry[...]
        stack[0:CHUNK, :] = x
        stack[CHUNK:, :] = low.astype(BF16)
        turned = rhs.astype(F32).T.astype(BF16)
        both = jnp.concatenate(
            [
                jnp.concatenate([gram, lhs], axis=1),
                jnp.concatenate([turned, jnp.zeros((turned.shape[0], lhs.shape[1]), BF16)], axis=1),
            ],
            axis=0,
        )
        result = jnp.dot(both, stack[...], preferred_element_type=F32)
        out[at, :] = (outer_ref[at, :] * (result[:CHUNK] + skip * x.astype(F32))).astype(BF16)
        carry[...] = second * (low + result[CHUNK:])
        cross = lax.dot_general(b_ref[at, :], stack[CHUNK:, :], NT, preferred_element_type=F32)
        small[at, :] = (small_local[at, :] + cross).astype(BF16)

    def rs_copy(which, k, j, c, peer):
        src = (rpart, wpart)[which]
        return pltpu.make_async_remote_copy(
            src_ref=src.at[rows_at(c, CHUNK)],
            dst_ref=got.at[which, k - 1, rows_at(j, CHUNK)],
            send_sem=rs_send.at[which, k - 1, j],
            recv_sem=rs_recv.at[which, k - 1, j],
            device_id={"tp": peer},
            device_id_type=MESH,
        )

    def send_part(which, c):
        peer = c // per
        k = lax.rem(peer - tp + ntp, ntp)

        @pl.when(k != 0)
        def _():
            rs_copy(which, k, c - peer * per, c, peer).start()

    def forward(c, stack):
        one(c, False, qbuf, kbuf, xs_ref, gs_ref, eb_ref, stack, tsum, mixed_ref, rpart, rlocal)

    def backward(c, stack):
        one(c, True, kbuf, qbuf, gs_ref, xs_ref, ea_ref, stack, csum, grad_ref, wpart, wlocal)

    def two_blocks(m, carry):
        i, j = 2 * m, chunks - 1 - 2 * m
        forward(i, fstack0)
        backward(j, bstack0)
        forward(i + 1, fstack1)
        backward(j - 1, bstack1)
        send_part(0, i)
        send_part(1, j)
        send_part(0, i + 1)
        send_part(1, j - 1)
        return carry

    lax.fori_loop(0, chunks // 2, two_blocks, 0)

    for which, (src, out) in enumerate(((rpart, rout), (wpart, wout))):
        total = src[own, :].astype(F32)
        for k in range(1, ntp):
            for j in range(per):
                rs_copy(which, k, j, 0, lax.rem(tp + k, ntp)).wait_recv()
            total = total + got[which, k - 1].astype(F32)
        out[...] = total.astype(BF16)

    for k in range(1, ntp):
        for which in range(2):
            ag_copy(which, k, tp).wait_send()
            for j in range(per):
                peer = lax.rem(tp + k, ntp)
                rs_copy(which, k, j, peer * per + j, peer).wait_send()

    for k in range(1, nseq):
        log_copy(k, seq).wait_send()
    for n in range(2):
        to_sibling(n, pair_out, pair_in, pair_send, pair_recv).wait_send()
        to_sibling(n, half_out, half_in, half_send, half_recv).wait_send()
    for k in range(1, groups):
        sum_copy(0, k, group).wait_send()


def local(nseq, ntp, head_inputs, write_keys, read_queries, log_decay, skip_gain, out_grad):
    tokens, width = head_inputs.shape
    rows, size = write_keys.shape
    heads = log_decay.shape[0]
    chunks = tokens // CHUNK
    vmem = pl.BlockSpec(memory_space=pltpu.VMEM)
    hbm = pl.BlockSpec(memory_space=pl.ANY)
    dma = pltpu.SemaphoreType.DMA
    big = pltpu.VMEM((tokens, width), BF16)
    part = pltpu.VMEM((rows, size), BF16)
    wide, tall = pltpu.VMEM((tokens, width), BF16), pltpu.VMEM((tokens, size), BF16)
    total = pltpu.VMEM((size, width), F32)
    halves = pltpu.VMEM((2, size // 2, width), BF16)
    small = pltpu.VMEM((tokens, size), F32)
    groups = nseq // 2
    lanes = -(-heads // LANES) * LANES
    outer = pltpu.VMEM((tokens, width), F32)
    stack = pltpu.VMEM((CHUNK + size, width), BF16)
    return pl.pallas_call(
        functools.partial(kernel, nseq, ntp),
        out_shape=(big, big, part, part),
        in_specs=[hbm, hbm, vmem, vmem, vmem, vmem],
        out_specs=[vmem] * 4,
        scratch_shapes=[wide] * 6
        + [tall, tall, total, total, pltpu.VMEM((4 * chunks, width), F32), outer, outer]
        + [pltpu.VMEM((nseq, 8, lanes), F32)]
        + [pltpu.VMEM((8 * groups, width), F32), pltpu.VMEM((16, width), F32)]
        + [halves, halves, halves, pltpu.VMEM((groups, size // 2, width), BF16), halves, halves]
        + [stack] * 4
        + [tall, tall, small, small, pltpu.VMEM((2, ntp - 1, rows, size), BF16)]
        + [dma((2, chunks)), dma((2, ntp)), dma((2, ntp)), dma((nseq,)), dma((nseq,))]
        + [dma((2,)), dma((2,)), dma((groups,)), dma((groups,)), dma((2,)), dma((2,))]
        + [dma((2, ntp - 1, rows // CHUNK))] * 2,
        compiler_params=pltpu.CompilerParams(
            collective_id=0, has_side_effects=True, vmem_limit_bytes=LIMIT
        ),
        name="ssd_layer",
    )(head_inputs, out_grad, write_keys, read_queries, log_decay, skip_gain[None, :])


def solution(mesh):
    in_specs = (
        P("seq", "tp"),
        P(("seq", "tp"), None),
        P(("seq", "tp"), None),
        P("tp", "seq"),
        P("tp"),
        P("seq", "tp"),
    )
    out_specs = (P("seq", "tp"), P("seq", "tp"), P(("seq", "tp"), None), P(("seq", "tp"), None))
    body = functools.partial(local, mesh.shape["seq"], mesh.shape["tp"])
    return jax.shard_map(body, mesh=mesh, in_specs=in_specs, out_specs=out_specs, check_vma=False)
```
